256 devices in a mesh: tm: 32 (over y_lo, z, core), stream: 8 (over y_hi, x).
Axes of the slice: x: 4, y: 4 (y_hi: 2, y_lo: 2; y = y_hi * 2 + y_lo), z: 8, core: 2. Of those that a mesh axis runs over, the one named last changes fastest.
Arguments:
- latents: bfloat16 [8, 8192, 512], P('stream', 'tm'), parts along dimension 0, may hold values from -6 to 6
- gain_attn: float32 [1, 512], replicated, may hold values from 0.5 to 1.5
- w_query: bfloat16 [1, 512, 512], replicated, may hold values from -8 to 8
- w_key: bfloat16 [1, 512, 512], replicated, may hold values from -8 to 8
- w_value: bfloat16 [1, 512, 512], replicated, may hold values from -0.25 to 0.25
- w_out: bfloat16 [1, 512, 512], replicated, may hold values from -0.25 to 0.25
- scale_attn: float32 [1, 512], replicated, may hold values from 0.3 to 1
- gain_ffn: float32 [1, 512], replicated, may hold values from 0.5 to 1.5
- w_up: bfloat16 [1, 512, 2048], replicated, may hold values from -0.25 to 0.25
- w_down: bfloat16 [1, 2048, 512], replicated, may hold values from -0.125 to 0.125
- scale_ffn: float32 [1, 512], replicated, may hold values from 0.3 to 1
- w_lift: bfloat16 [7, 512, 1024], P(None, None, 'tm'), may hold values from -0.09375 to 0.09375
- bias_lift: float32 [1024], replicated, may hold values from -2 to 2
- w_upsample: bfloat16 [1024, 8192], P(None, 'tm'), may hold values from -0.125 to 0.125
- bias_upsample: float32 [512], replicated, may hold values from -2 to 2
- w_conv_first: bfloat16 [512, 768], replicated, may hold values from -0.15625 to 0.15625
- bias_first: float32 [256], replicated, may hold values from -2 to 2
- w_conv_second: bfloat16 [256, 512], replicated, may hold values from -0.375 to 0.375
- bias_second: float32 [512], replicated, may hold values from -2 to 2
Outputs:
- audio_features: bfloat16 [8, 65536, 512], P('stream', 'tm'), parts along dimension 0
The draws below stay inside these ranges and needn't reach their ends.
There are 8 independent parts, one for each index of `stream`. The reference program is written for one: setup_inputs(seed, part) draws one part's arguments, and reference() takes and returns one part's arrays. A program takes and returns all parts, laid end to end along the dimension named above; an argument that names none is the same for every part. Nothing has to cross between parts.
All inputs are finite; a program needn't handle non-finite values.
Results may differ from the reference program's by a relative error of at most 0.015.
Values may be sent and summed in bfloat16 or wider, within the bound.
A program may use at most 128 MiB of HBM per device.

```python
import math
import jax
import jax.numpy as jnp
from jax import lax

D = 512
HEADS = 8
HEAD_DIM = 64
FF = 2048
LAYERS = 1
WIN = 250
UPS = 8
C0 = 1024
C1 = 512
CH = 256
STREAMS = 1
FRAMES_DEV = 256
FRAMES = 8192
N_TM = 32


def shared_draw(key):
    return jax.random.truncated_normal(key, -4.0, 4.0, (LAYERS, D, D), jnp.float32) / math.sqrt(D)


def draw_w_query(key, part):
    shared = shared_draw(key)
    return jnp.clip(shared, -8.0, 8.0).astype(jnp.bfloat16)


def draw_w_key(key, part):
    key = jax.random.fold_in(key, 2)
    matrix = jax.random.truncated_normal(key, -4.0, 4.0, (LAYERS, D, D), jnp.float32) / math.sqrt(D)
    return jnp.clip(matrix, -8.0, 8.0).astype(jnp.bfloat16)


def shard_levels(key, shape, cuts, low, high):
    def one(dim, blocks):
        heights = jax.random.uniform(jax.random.fold_in(jax.random.fold_in(key, 6), dim), (blocks,), jnp.float32, low / len(cuts), high / len(cuts))
        return jnp.repeat(jnp.exp(heights), shape[dim] // blocks).reshape((-1,) + (1,) * (len(shape) - dim - 1))

    gain = one(*cuts[0])
    for cut in cuts[1:]:
        gain = gain * one(*cut)
    return gain


def bell_draw(own_key, dims, deviation, most, cuts=(), kind=jnp.bfloat16):
    drawn = deviation * jax.random.normal(own_key, dims, jnp.float32)
    if cuts:
        drawn = drawn * shard_levels(own_key, dims, cuts, -0.22, 0.18)
    return jnp.clip(drawn, -most, most).astype(kind)


def setup_inputs(seed: int = 0, part: int = 0) -> dict:
    splits = jax.random.split(jax.random.key(seed), 20)
    part_splits = jax.random.split(jax.random.fold_in(splits[19], part), 20)
    return {
        "latents": bell_draw(part_splits[0], (STREAMS, FRAMES, D), 1.0, 6.0, ((1, 32),)),
        "gain_attn": jnp.clip(1.0 + 0.1 * jax.random.normal(splits[1], (LAYERS, D), jnp.float32), 0.5, 1.5),
        "w_query": draw_w_query(jax.random.fold_in(splits[19], 71), part),
        "w_key": draw_w_key(jax.random.fold_in(splits[19], 71), part),
        "w_value": bell_draw(splits[4], (LAYERS, D, D), D ** -0.5, 0.25),
        "w_out": bell_draw(splits[5], (LAYERS, D, D), D ** -0.5, 0.25),
        "scale_attn": jnp.clip(jax.random.uniform(splits[6], (LAYERS, D), jnp.float32, 0.3, 1.0), 0.3, 1.0),
        "gain_ffn": jnp.clip(1.0 + 0.1 * jax.random.normal(splits[7], (LAYERS, D), jnp.float32), 0.5, 1.5),
        "w_up": bell_draw(splits[8], (LAYERS, D, FF), D ** -0.5, 0.25),
        "w_down": bell_draw(splits[9], (LAYERS, FF, D), FF ** -0.5, 0.125),
        "scale_ffn": jnp.clip(jax.random.uniform(splits[10], (LAYERS, D), jnp.float32, 0.3, 1.0), 0.3, 1.0),
        "w_lift": bell_draw(splits[11], (7, D, C0), (7 * D) ** -0.5, 0.09375, ((2, 32),)),
        "bias_lift": bell_draw(splits[12], (C0,), 0.3, 2.0, (), jnp.float32),
        "w_upsample": bell_draw(splits[13], (C0, 2 * UPS * C1), (2 * C0) ** -0.5, 0.125, ((1, 32),)),
        "bias_upsample": bell_draw(splits[14], (C1,), 0.3, 2.0, (), jnp.float32),
        "w_conv_first": bell_draw(splits[15], (C1, 3 * CH), (3 * C1) ** -0.5, 0.15625),
        "bias_first": bell_draw(splits[16], (CH,), 0.3, 2.0, (), jnp.float32),
        "w_conv_second": bell_draw(splits[17], (CH, C1), CH ** -0.5, 0.375),
        "bias_second": bell_draw(splits[18], (C1,), 0.3, 2.0, (), jnp.float32),
    }


def layer_norm(values_in, gain_row):
    average = lax.optimization_barrier(jnp.mean(values_in, axis=-1, keepdims=True))
    centred = values_in - average
    variance = lax.optimization_barrier(jnp.mean(centred * centred, axis=-1, keepdims=True))
    return centred * lax.rsqrt(variance + 1e-05) * gain_row

def rotate(tensor, positions):
    half_size = tensor.shape[-1] // 2
    frequency = jnp.exp(-jnp.log(10000.0) * jnp.arange(half_size, dtype=jnp.float32) / half_size)
    angles = positions.astype(jnp.float32)[:, None] * frequency[None, :]
    cosine = jnp.cos(angles)[:, None, :]
    sine_part = jnp.sin(angles)[:, None, :]
    front_half = tensor[..., :half_size]
    back_half = tensor[..., half_size:]
    return jnp.concatenate([front_half * cosine - back_half * sine_part, front_half * sine_part + back_half * cosine], axis=-1)

def heads_of(normed, weight, positions, rotated):
    projected = jnp.dot(normed, weight, preferred_element_type=jnp.float32)
    projected = projected.reshape(projected.shape[:-1] + (HEADS, HEAD_DIM))
    if rotated:
        projected = rotate(projected, positions)
    return projected.astype(jnp.bfloat16)

def attend(query_rows, key_rows, value_rows, query_pos, key_pos):
    scores = jnp.einsum('sqhd,skhd->shqk', query_rows.astype(jnp.float32), key_rows.astype(jnp.float32)) / jnp.sqrt(jnp.float32(HEAD_DIM))
    allowed = (key_pos[None, :] <= query_pos[:, None]) & (key_pos[None, :] > query_pos[:, None] - WIN) & (key_pos[None, :] >= 0)
    scores = jnp.where(allowed, scores, -1e+30)
    row_max = lax.optimization_barrier(jnp.max(scores, axis=-1, keepdims=True))
    weights = jnp.where(allowed, jnp.exp(scores - row_max), 0.0)
    probs = (weights / lax.optimization_barrier(jnp.sum(weights, axis=-1, keepdims=True))).astype(jnp.bfloat16)
    mixed = jnp.einsum('shqk,skhd->sqhd', probs.astype(jnp.float32), value_rows.astype(jnp.float32))
    return mixed.astype(jnp.bfloat16)

def reference(latents, gain_attn, w_query, w_key, w_value, w_out, scale_attn, gain_ffn, w_up, w_down, scale_ffn, w_lift, bias_lift, w_upsample, bias_upsample, w_conv_first, bias_first, w_conv_second, bias_second):
    length = FRAMES
    positions = jnp.arange(length, dtype=jnp.int32)
    current = latents
    for layer_id in range(LAYERS):
        state = current.astype(jnp.float32)
        normed = layer_norm(state, gain_attn[layer_id]).astype(jnp.bfloat16)
        query_rows = heads_of(normed, w_query[layer_id], positions, True)
        key_rows = heads_of(normed, w_key[layer_id], positions, True)
        value_rows = heads_of(normed, w_value[layer_id], positions, False)
        key_pad = jnp.pad(key_rows, ((0, 0), (WIN, 0), (0, 0), (0, 0)))
        value_pad = jnp.pad(value_rows, ((0, 0), (WIN, 0), (0, 0), (0, 0)))

        def block_attend(block_index):
            anchor = (block_index * FRAMES_DEV).astype(jnp.int32)
            query_block = lax.dynamic_slice_in_dim(query_rows, anchor, FRAMES_DEV, 1)
            key_block = lax.dynamic_slice_in_dim(key_pad, anchor, FRAMES_DEV + WIN, 1)
            value_block = lax.dynamic_slice_in_dim(value_pad, anchor, FRAMES_DEV + WIN, 1)
            query_pos = anchor + jnp.arange(FRAMES_DEV, dtype=jnp.int32)
            key_pos = anchor - WIN + jnp.arange(FRAMES_DEV + WIN, dtype=jnp.int32)
            return attend(query_block, key_block, value_block, query_pos, key_pos)
        blocks = lax.map(block_attend, jnp.arange(N_TM, dtype=jnp.int32))
        mixed = jnp.moveaxis(blocks, 0, 1).reshape(STREAMS, length, D)
        residual = state + scale_attn[layer_id] * jnp.dot(mixed, w_out[layer_id], preferred_element_type=jnp.float32)
        normed_two = layer_norm(residual, gain_ffn[layer_id]).astype(jnp.bfloat16)
        hidden = jax.nn.gelu(jnp.dot(normed_two, w_up[layer_id], preferred_element_type=jnp.float32), approximate=False).astype(jnp.bfloat16)
        current = (residual + scale_ffn[layer_id] * jnp.dot(hidden, w_down[layer_id], preferred_element_type=jnp.float32)).astype(jnp.bfloat16)
    lift_pad = jnp.pad(current, ((0, 0), (6, 0), (0, 0)))
    lifted = jnp.zeros((STREAMS, length, C0), jnp.float32) + bias_lift
    for tap_id in range(7):
        lifted = lifted + jnp.dot(lift_pad[:, tap_id:tap_id + length], w_lift[tap_id], preferred_element_type=jnp.float32)
    activated = jax.nn.elu(lifted).astype(jnp.bfloat16)
    tap_terms = jnp.dot(activated, w_upsample, preferred_element_type=jnp.float32).reshape(STREAMS, length, 2, UPS, C1)
    earlier = jnp.concatenate([jnp.zeros((STREAMS, 1, UPS, C1), jnp.float32), tap_terms[:, :-1, 1]], axis=1)
    upsampled = (bias_upsample + tap_terms[:, :, 0] + earlier).reshape(STREAMS, length * UPS, C1).astype(jnp.bfloat16)
    rectified = jax.nn.elu(upsampled.astype(jnp.float32)).astype(jnp.bfloat16)
    padded = jnp.pad(rectified, ((0, 0), (2, 0), (0, 0)))
    conv_terms = jnp.dot(padded, w_conv_first, preferred_element_type=jnp.float32).reshape(STREAMS, length * UPS + 2, 3, CH)
    squeezed = jax.nn.elu(bias_first + conv_terms[:, :-2, 0] + conv_terms[:, 1:-1, 1] + conv_terms[:, 2:, 2]).astype(jnp.bfloat16)
    output = upsampled.astype(jnp.float32) + bias_second + jnp.dot(squeezed, w_conv_second, preferred_element_type=jnp.float32)
    return output.astype(jnp.bfloat16)
```

```python
import functools
import math

import jax
import jax.numpy as jnp
import numpy as np
from jax import lax
from jax.experimental import pallas as pl
from jax.experimental.pallas import tpu as pltpu
from jax.sharding import PartitionSpec as P

MESH = pl.DeviceIdType.MESH
BF16, F32 = jnp.bfloat16, jnp.float32
HEADS, HEAD_DIM, WIN, UPS = 8, 64, 250, 8
FRAMES, D, FF, C0, C1, CH = 256, 512, 2048, 1024, 512, 256
HALO = 272
ROWS = HALO + FRAMES
LIVE = 272
LEAD = LIVE - FRAMES


def coords():
    t = lax.axis_index("tm")
    s = lax.axis_index("stream")
    return s % 4, (s // 4) * 2 + t // 16, (t // 2) % 8, t % 2


def device(x, y, z, c):
    return ((y % 2) * 16 + z * 2 + c, (y // 2) * 4 + x)


class Gather:
    def __init__(self, wl, wu, lbuf, ubuf, send_sems, recv_sems):
        self.x, self.y, self.z, self.c = x, y, z, c = coords()
        self.xp = self.x % 2
        self.src = {"L": wl, "U": wu}
        self.buf = {"L": lbuf, "U": ubuf}
        self.send_sems, self.recv_sems = send_sems, recv_sems
        self.sent = []
        self.to = {
            "z+": device(x, y, (z + 1) % 8, c),
            "z-": device(x, y, (z + 7) % 8, c),
            "y+": device(x, (y + 1) % 4, z, c),
            "y-": device(x, (y + 3) % 4, z, c),
            "x+": device((x + 1) % 4, y, z, c),
            "x-": device((x + 3) % 4, y, z, c),
            "s": device(x, y, z, 1 - c),
        }
        t, s = lax.axis_index("tm"), lax.axis_index("stream")
        self.after = [((t + k) % 32, s) for k in (1, 2)]
        self.before = [((t + 32 - k) % 32, s) for k in (1, 2)]

    def span(self, kind, part):
        xp = self.xp
        if kind == "L":
            return {
                "W": (0, 7),
                "P": (2 * xp, 5),
                "P0": (2 * xp, 3),
                "P1": (2 * xp + 3, 2),
                "M": (5 * xp, 2),
                "O": (5 - 5 * xp, 2),
            }[part]
        start, size = {
            "W": (0, 1024),
            "P": (336 * xp, 688),
            "P0": (336 * xp, 352),
            "P1": (336 * xp + 352, 336),
            "M": (688 * xp, 336),
            "O": (688 - 688 * xp, 336),
        }[part]
        return (start if isinstance(start, int) else pl.multiple_of(start, 16)), size

    def ref(self, kind, row, d, part, core=None, own=False):
        start, size = self.span(kind, part)
        if own:
            return self.src[kind].at[pl.ds(start, size)]
        yl, zz = (self.y + row) % 2, (self.z + d + 8) % 8
        core = self.c if core is None else core
        if kind == "U":
            return self.buf[kind].at[yl, zz, core, pl.ds(start, size)]
        first = pl.multiple_of(32 * (yl * 16 + zz * 2 + core), 32)
        return self.buf[kind].at[pl.ds(start, size), pl.ds(first, 32)]

    def start(self, src, dst, target, recv):
        copy = pltpu.make_async_remote_copy(
            src_ref=src,
            dst_ref=dst,
            send_sem=self.send_sems.at[len(self.sent)],
            recv_sem=self.recv_sems.at[recv],
            device_id=target,
            device_id_type=MESH,
        )
        copy.start()
        self.sent.append(copy)

    def send(self, kind, row, d, part, where, recv):
        src = self.ref(kind, row, d, part, own=row == 0 and d == 0)
        self.start(src, self.ref(kind, row, d, part), self.to[where], recv)

    def wait(self, ref, recv):
        pltpu.make_async_remote_copy(
            src_ref=ref,
            dst_ref=ref,
            send_sem=self.send_sems.at[0],
            recv_sem=self.recv_sems.at[recv],
            device_id=self.to["s"],
            device_id_type=MESH,
        ).wait_recv()

    def wait_part(self, kind, row, d, part, recv, core=None):
        self.wait(self.ref(kind, row, d, part, core=core), recv)

    @staticmethod
    def sem(what, kind, row, d):
        base = 50 * (kind == "U")
        if what == "P1":
            return base + 48 + row
        return base + {"P": 0, "O": 16, "S": 32}[what] + row * 8 + d + 3

    def part_p(self, kind, row, d):
        sem = self.sem
        if row or d:
            if (row, d) in ((0, 4), (1, 0)):
                self.wait_part(kind, row, d, "P0", sem("P", kind, row, d))
                self.wait_part(kind, row, d, "P1", sem("P1", kind, row, d))
            else:
                self.wait_part(kind, row, d, "P", sem("P", kind, row, d))
        if row == 0:
            if d in (0, -1, -2):
                self.send(kind, 0, d, "P", "z+", sem("P", kind, 0, d - 1))
            if d in (0, 1, 2):
                self.send(kind, 0, d, "P", "z-", sem("P", kind, 0, d + 1))
            if d == -3:
                self.send(kind, 0, d, "P0", "z+", sem("P", kind, 0, 4))
            if d == 3:
                self.send(kind, 0, d, "P1", "z-", sem("P1", kind, 0, 4))
            if d == 0:
                self.send(kind, 0, 0, "P0", "y+", sem("P", kind, 1, 0))
                self.send(kind, 0, 0, "P1", "y-", sem("P1", kind, 1, 0))
                self.send(kind, 0, 0, "W", "s", sem("S", kind, 0, 0))
            else:
                self.send(kind, 0, d, "P", "y+" if d in (1, -2, 3) else "y-", sem("P", kind, 1, d))
        if row or d:
            self.send(kind, row, d, "M", "x+" if (d + row) % 2 else "x-", sem("O", kind, row, d))

    def part_o(self, kind, row, d):
        if row or d:
            self.wait_part(kind, row, d, "O", self.sem("O", kind, row, d))
            self.send(kind, row, d, "W", "s", self.sem("S", kind, row, d))

    def from_other_core(self, kind, row, d):
        self.wait_part(kind, row, d, "W", self.sem("S", kind, row, d), core=1 - self.c)

    def barrier(self):
        semaphore = pltpu.get_barrier_semaphore()
        targets = list(self.to.values()) + self.before
        for target in targets:
            pl.semaphore_signal(semaphore, inc=1, device_id=target, device_id_type=MESH)
        pl.semaphore_wait(semaphore, len(targets))

    def finish(self):
        for copy in self.sent:
            copy.wait_send()


def dot(a, b):
    return jnp.dot(a, b, preferred_element_type=F32)


def dot_nt(a, b):
    return lax.dot_general(a, b, (((1,), (1,)), ((), ())), preferred_element_type=F32)


def elu(v):
    return jnp.where(v > 0, v, jnp.exp(jnp.minimum(v, 0.0)) - 1.0)


def layer_norm(v, gain):
    centred = v - jnp.mean(v, axis=-1, keepdims=True)
    variance = jnp.mean(centred * centred, axis=-1, keepdims=True)
    return centred * lax.rsqrt(variance + 1e-05) * gain


def kernel(
    lat, ga, wq, wk, wv, wo, sa, gf, wup, wdn, sf, wl, bl, wu, bu, wc1, b1, wc2, b2, near, far,
    out,
    lbuf, ubuf, xin, vproj, vup, vdn, vc1, vc2, vga, vsa, vgf, vsf, vbl, vbu, vb1, vb2, vnear, vfar,
    qs, ks, vs, mixed, res, nrm, ffacc, cur7, act2, rect, summed, obf,
    send_sems, recv_sems, here_sems, out_sems,
):
    g = Gather(wl, wu, lbuf, ubuf, send_sems, recv_sems)
    t = lax.axis_index("tm")
    here = []

    def bring(src, dst):
        copy = pltpu.make_async_copy(src, dst, here_sems.at[len(here)])
        copy.start()
        here.append(copy)
        return copy

    own_x = bring(lat, xin.at[pl.ds(HALO, FRAMES)])
    g.barrier()
    g.start(lat, xin.at[pl.ds(LEAD, FRAMES)], g.after[0], 100)
    g.start(lat.at[pl.ds(FRAMES - LEAD, LEAD)], xin.at[pl.ds(0, LEAD)], g.after[1], 101)
    g.part_p("L", 0, 0)
    in_ga, in_near, in_far = bring(ga, vga), bring(near, vnear), bring(far, vfar)
    in_proj = [bring(w, vproj.at[i]) for i, w in enumerate((wk, wv, wq, wo))]
    g.part_p("U", 0, 0)
    own_l = bring(wl, g.ref("L", 0, 0, "W"))
    own_u = bring(wu, g.ref("U", 0, 0, "W"))
    in_up, in_dn = bring(wup, vup), bring(wdn, vdn)
    in_vec = [
        bring(a, b)
        for a, b in ((sa, vsa), (gf, vgf), (sf, vsf), (bl, vbl), (bu, vbu), (b1, vb1), (b2, vb2))
    ]
    in_c1, in_c2 = bring(wc1, vc1), bring(wc2, vc2)

    def keys_and_queries():
        own_x.wait()
        g.wait(xin.at[pl.ds(LEAD, FRAMES)], 100)
        g.wait(xin.at[pl.ds(0, LEAD)], 101)
        for copy in (in_ga, in_near, in_far, *in_proj):
            copy.wait()
        x = xin[...].astype(F32)
        normed = layer_norm(x, vga[...]).astype(BF16)
        cos_a, sin_a = vfar[0, pl.ds(t, 1), :], vfar[1, pl.ds(t, 1), :]
        cos_b, sin_b = vnear[0], vnear[1]
        cosine, sine = cos_a * cos_b - sin_a * sin_b, sin_a * cos_b + cos_a * sin_b
        lane = lax.broadcasted_iota(jnp.int32, (1, 128), 1)
        first = lane % 64 < 32
        sine = jnp.where(first, -sine, sine)

        def rope(v, cosine, sine):
            parts = []
            for i in range(4):
                block = v[:, 128 * i : 128 * i + 128]
                other = jnp.where(first, pltpu.roll(block, 96, 1), pltpu.roll(block, 32, 1))
                parts.append(block * cosine + other * sine)
            return jnp.concatenate(parts, axis=1).astype(BF16)

        ks[...] = rope(dot(normed, vproj[0]), cosine, sine)
        vs[...] = dot(normed, vproj[1]).astype(BF16)
        tail = ROWS - LIVE
        qs[...] = rope(dot(normed[tail:], vproj[2]), cosine[tail:], sine[tail:]) * BF16(0.125)

    def attention(pair):
        lanes = slice(128 * pair, 128 * pair + 128)
        low = lax.broadcasted_iota(jnp.int32, (1, 128), 1) < 64
        for q0, size, k0, width in ((256, 96, 0, 352), (352, 96, 96, 352), (448, 80, 192, 336)):
            q_row = q0 + lax.broadcasted_iota(jnp.int32, (size, width), 0)
            k_row = k0 + lax.broadcasted_iota(jnp.int32, (size, width), 1)
            allowed = (k_row <= q_row) & (k_row > q_row - WIN) & (k_row >= HALO - FRAMES * t)
            q = qs[q0 - 256 : q0 - 256 + size, lanes]
            k, v = ks[k0 : k0 + width, lanes], vs[k0 : k0 + width, lanes]
            halves = []
            for mask in (low, ~low):
                scores = jnp.where(allowed, dot_nt(jnp.where(mask, q, BF16(0)), k), -1e30)
                weights = jnp.exp(scores - jnp.max(scores, axis=-1, keepdims=True))
                weights = jnp.where(allowed, weights, 0.0)
                total = jnp.maximum(jnp.sum(weights, axis=-1, keepdims=True), 0.5)
                halves.append(dot((weights / total).astype(BF16), v))
            mixed[q0 - 256 : q0 - 256 + size, lanes] = jnp.where(low, *halves).astype(BF16)

    def after_attention():
        for copy in in_vec:
            copy.wait()
        state = xin[ROWS - LIVE :, :].astype(F32)
        residual = state + vsa[...] * dot(mixed[...], vproj[3])
        res[...] = residual
        nrm[...] = layer_norm(residual, vgf[...]).astype(BF16)
        in_up.wait()
        in_dn.wait()

    def feed_forward(i):
        cols = slice(512 * i, 512 * i + 512)
        v = dot(nrm[...], vup[:, cols])
        hidden = (0.5 * v * (1.0 + lax.erf(v * (1.0 / math.sqrt(2.0))))).astype(BF16)
        part = dot(hidden, vdn[cols, :])
        ffacc[...] = part if i == 0 else ffacc[...] + part

    live_row = lax.broadcasted_iota(jnp.int32, (LIVE, 1), 0)
    real = (live_row >= LEAD) | (t > 0)

    def layer_end():
        current = (res[...] + vsf[...] * ffacc[...]).astype(BF16).astype(F32)
        current = jnp.where(real, current, 0.0)
        for m in range(7):
            moved = pltpu.roll(current, 6 - m, 0) if m < 6 else current
            cur7[:, 512 * m : 512 * m + 512] = moved.astype(BF16)

    def lift(i):
        cols = slice(256 * i, 256 * i + 256)
        total = vbl[:, cols]
        for m in range(7):
            total = total + dot_nt(cur7[:, 512 * m : 512 * m + 512], lbuf[m, cols, :])
        active = jnp.where(real, elu(total), 0.0).astype(BF16)
        act2[:, cols] = active
        act2[:, C0 + 256 * i : C0 + 256 * i + 256] = pltpu.roll(active.astype(F32), 1, 0).astype(BF16)

    def upsample(d):
        j = (g.z + d + 8) % 8
        halves = []
        for half in range(2):
            cols = slice(256 * half, 256 * half + 256)
            up = dot(act2[:, :C0], ubuf[0, j, half]) + dot(act2[:, C0:], ubuf[1, j, half])
            up = (up + vbu[:, cols]).astype(BF16).astype(F32)
            halves.append(up)
        up = jnp.concatenate(halves, axis=1)
        kept = up[LEAD:] + vb2[...]
        for i in range(4):
            summed[i, pl.ds(j, FRAMES, stride=UPS), :] = kept[:, 128 * i : 128 * i + 128]
        rectified = jnp.where(real, elu(up), 0.0)
        rect[j + 2] = rectified.astype(BF16)

        @pl.when(j >= 6)
        def _():
            rect[j - 6] = pltpu.roll(rectified, 1, 0).astype(BF16)

    def residual_unit(d):
        j = (g.z + d + 8) % 8
        total = vb1[...]
        for m in range(3):
            total = total + dot(rect[j + m, LEAD:], vc1[:, CH * m : CH * m + CH])
        second = dot(elu(total).astype(BF16), vc2[...])
        rows = pl.ds(j, FRAMES, stride=UPS)
        for i in range(4):
            summed[i, rows, :] = summed[i, rows, :] + second[:, 128 * i : 128 * i + 128]

    def p(kind, row, *ds):
        for d in ds:
            g.part_p(kind, row, d)

    def o(kind, *ds, rows=(0, 1)):
        for d in ds:
            for row in rows:
                g.part_o(kind, row, d)

    def whole(kind, *ds):
        for d in ds:
            for row in (0, 1):
                g.from_other_core(kind, row, d)

    keys_and_queries()
    p("L", 0, -1, 1)
    p("L", 1, 0)
    attention(0)
    attention(1)
    p("L", 0, -2, 2)
    p("L", 1, -1, 1)
    o("L", 0, rows=(1,))
    attention(2)
    attention(3)
    p("U", 0, -1, 1)
    p("U", 1, 0)
    p("L", 0, -3, 3)
    p("L", 1, -2, 2)
    o("L", -1, 1)
    after_attention()
    feed_forward(0)
    feed_forward(1)
    p("L", 0, 4)
    p("L", 1, -3, 3)
    o("L", -2, 2)
    feed_forward(2)
    feed_forward(3)
    p("U", 0, -2, 2)
    p("U", 1, -1, 1)
    o("U", 0, rows=(1,))
    p("L", 1, 4)
    o("L", -3, 3)
    layer_end()
    o("L", 4)
    whole("L", 0, -1, 1, -2, 2, -3, 3, 4)
    own_l.wait()
    for i in range(4):
        lift(i)
    p("U", 0, -3, 3)
    p("U", 1, -2, 2)
    o("U", -1, 1)
    own_u.wait()
    for copy in (in_c1, in_c2):
        copy.wait()
    whole("U", 0)
    upsample(0)
    whole("U", -1, 1)
    p("U", 0, 4)
    p("U", 1, -3, 3)
    o("U", -2, 2)
    upsample(-1)
    upsample(1)
    residual_unit(1)
    p("U", 1, 4)
    o("U", -3, 3)
    whole("U", -2, 2)
    upsample(-2)
    upsample(2)
    residual_unit(0)
    residual_unit(2)
    o("U", 4)
    whole("U", -3, 3)
    upsample(-3)
    upsample(3)
    residual_unit(-1)
    residual_unit(3)
    whole("U", 4)
    upsample(4)
    residual_unit(4)
    residual_unit(-2)
    residual_unit(-3)
    leaving = []
    for i in range(4):
        rows = pl.ds(512 * i, 512)
        for k in range(4):
            obf[rows, 128 * k : 128 * k + 128] = summed[k, rows, :].astype(BF16)
        copy = pltpu.make_async_copy(obf.at[rows], out.at[rows], out_sems.at[i])
        copy.start()
        leaving.append(copy)
    for copy in leaving:
        copy.wait()

    g.finish()


def tables():
    frequency = 10000.0 ** (-np.arange(32, dtype=np.float64) / 32)
    frequency = np.tile(frequency, 4)[None, :]

    def both(frames):
        angles = frames[:, None] * frequency
        return np.stack([np.cos(angles), np.sin(angles)]).astype(np.float32)

    return both(np.arange(ROWS) - float(HALO)), both(np.arange(32) * float(FRAMES))


def body(
    latents, gain_attn, w_query, w_key, w_value, w_out, scale_attn, gain_ffn, w_up, w_down, scale_ffn,
    w_lift, bias_lift, w_upsample, bias_upsample, w_conv_first, bias_first, w_conv_second, bias_second,
):
    near, far = tables()
    operands = (
        latents[0], gain_attn, w_query[0], w_key[0], w_value[0], w_out[0], scale_attn, gain_ffn, w_up[0], w_down[0],
        scale_ffn, jnp.transpose(w_lift, (0, 2, 1)), bias_lift[None], w_upsample, bias_upsample[None], w_conv_first,
        bias_first[None], w_conv_second, bias_second[None], jnp.asarray(near), jnp.asarray(far),
    )
    vmem = pltpu.VMEM
    result = pl.pallas_call(
        kernel,
        out_shape=jax.ShapeDtypeStruct((FRAMES * UPS, C1), BF16),
        in_specs=[pl.BlockSpec(memory_space=pl.ANY)] * len(operands),
        out_specs=pl.BlockSpec(memory_space=pl.ANY),
        scratch_shapes=[
            vmem((7, C0, D), BF16),
            vmem((2, UPS, 2, C0, C1 // 2), BF16),
            vmem((ROWS, D), BF16),
            vmem((4, D, D), BF16),
            vmem((D, FF), BF16),
            vmem((FF, D), BF16),
            vmem((C1, 3 * CH), BF16),
            vmem((CH, C1), BF16),
            vmem((1, D), F32),
            vmem((1, D), F32),
            vmem((1, D), F32),
            vmem((1, D), F32),
            vmem((1, C0), F32),
            vmem((1, C1), F32),
            vmem((1, CH), F32),
            vmem((1, C1), F32),
            vmem((2, ROWS, 128), F32),
            vmem((2, 32, 128), F32),
            vmem((LIVE, D), BF16),
            vmem((ROWS, D), BF16),
            vmem((ROWS, D), BF16),
            vmem((LIVE, D), BF16),
            vmem((LIVE, D), F32),
            vmem((LIVE, D), BF16),
            vmem((LIVE, D), F32),
            vmem((LIVE, 7 * D), BF16),
            vmem((LIVE, 2 * C0), BF16),
            vmem((UPS + 2, LIVE, C1), BF16),
            vmem((4, FRAMES * UPS, 128), F32),
            vmem((FRAMES * UPS, C1), BF16),
            pltpu.SemaphoreType.DMA((112,)),
            pltpu.SemaphoreType.DMA((102,)),
            pltpu.SemaphoreType.DMA((24,)),
            pltpu.SemaphoreType.DMA((4,)),
        ],
        compiler_params=pltpu.CompilerParams(collective_id=0, has_side_effects=True, vmem_limit_bytes=60 * 2**20),
        cost_estimate=pl.CostEstimate(flops=11 * 10**9, bytes_accessed=36 * 10**6, transcendentals=4 * 10**6),
    )(*operands)
    return result[None]


def solution(mesh):
    whole = P()
    placed = [whole] * 19
    placed[0] = P("stream", "tm", None)
    placed[11] = P(None, None, "tm")
    placed[13] = P(None, "tm")
    return jax.shard_map(
        body, mesh=mesh, in_specs=tuple(placed), out_specs=P("stream", "tm", None), check_vma=False
    )
```

```python
import math

import jax
import jax.numpy as jnp
import numpy as np
from jax import lax
from jax.experimental import pallas as pl
from jax.experimental.pallas import tpu as pltpu
from jax.sharding import PartitionSpec as P

MESH = pl.DeviceIdType.MESH
BF16, F32 = jnp.bfloat16, jnp.float32
WIN, UPS = 250, 8
FRAMES, D, FF, C0, C1, CH = 256, 512, 2048, 1024, 512, 256
HALO = 272
ROWS = HALO + FRAMES
LIVE = 272
LEAD = LIVE - FRAMES


def coords():
    t = lax.axis_index("tm")
    s = lax.axis_index("stream")
    return s % 4, (s // 4) * 2 + t // 16, (t // 2) % 8, t % 2


def device(x, y, z, c):
    return ((y % 2) * 16 + z * 2 + c, (y // 2) * 4 + x)


SPANS = {
    "L": {
        "W": (0, 0, 7), "C": (2, 2, 3), "Ca": (2, 2, 2), "Cb": (4, 4, 1), "M": (0, 5, 2), "Ma": (0, 5, 1),
        "Mb": (1, 6, 1), "O": (5, 0, 2), "Oa": (5, 0, 1), "Ob": (6, 1, 1),
    },
    "U": {
        "W": (0, 0, 1024), "C": (336, 336, 352), "Ca": (336, 336, 176), "Cb": (512, 512, 176), "M": (0, 688, 336),
        "Ma": (0, 688, 176), "Mb": (176, 864, 160), "O": (688, 0, 336), "Oa": (688, 0, 176), "Ob": (864, 176, 160),
    },
}
NEAR = (-1, 1, -2, 2, -3, 3)


def routes():
    sends, joins = {}, {}
    for kind in "LU":

        def add(part, row, d, *items):
            got = sends.setdefault((kind, part, row, d), [])
            for name, to_row, to_d, sent, link in items:
                got.append(((kind, name, to_row, to_d), sent, link))

        for q in "MC":
            add("W", 0, 0, (q, 0, -1, q, "z+"), (q, 0, 1, q, "z-"))
        add("W", 0, 0, ("M", 1, 0, "M", "y+"), ("C", 1, 0, "C", "y-"), ("S", 0, 0, "W", "s"))
        add("M", 1, 0, ("Oa", 1, 0, "Ma", "x+"), ("Ob", 1, 0, "Mb", "x-"))
        joins[kind, 1, 0] = ("M", "C", "Oa", "Ob")
        for d in NEAR:
            up, swap = d < 0, d in (-1, 2, -3)
            for q in "MC":
                if abs(d) < 3:
                    add(q, 0, d, (q, 0, d - 1 if up else d + 1, q, "z+" if up else "z-"))
                elif up == (q == "M"):
                    add(q, 0, d, (q, 0, 4, q, "z+" if up else "z-"))
                add(q, 0, d, (q, 1, d, q, "y+" if swap == (q == "M") else "y-"))
            add("M", 0, d, ("O", 0, d, "M", "x+" if swap else "x-"))
            add("M", 1, d, ("O", 1, d, "M", "x-" if swap else "x+"))
            joins[kind, 0, d] = joins[kind, 1, d] = ("M", "C", "O")
        for h, y, x in (("a", "y+", "x+"), ("b", "y-", "x-")):
            add("M", 0, 4, ("M" + h, 1, 4, "M" + h, y), ("O" + h, 0, 4, "M" + h, x))
            add("C", 0, 4, ("C" + h, 1, 4, "C" + h, y))
            add("M" + h, 1, 4, ("O" + h, 1, 4, "M" + h, x))
        joins[kind, 0, 4] = ("M", "C", "Oa", "Ob")
        joins[kind, 1, 4] = ("Ma", "Mb", "Ca", "Cb", "Oa", "Ob")
    return sends, joins


class Gather:
    def __init__(self, wl, wu, lbuf, ubuf, send_sems, recv_sems):
        self.x, self.y, self.z, self.c = x, y, z, c = coords()
        self.xp = self.x % 2
        self.src = {"L": wl, "U": wu}
        self.buf = {"L": lbuf, "U": ubuf}
        self.send_sems, self.recv_sems = send_sems, recv_sems
        self.sent = []
        self.sends, self.joins = routes()
        arrivals = [to for sends in self.sends.values() for to, _, _ in sends]
        arrivals += [(kind, "S", row, d) for kind, row, d in self.joins]
        self.number = {to: i + 2 for i, to in enumerate(arrivals)}
        self.here = set()
        self.to = {
            "z+": device(x, y, (z + 1) % 8, c),
            "z-": device(x, y, (z + 7) % 8, c),
            "y+": device(x, (y + 1) % 4, z, c),
            "y-": device(x, (y + 3) % 4, z, c),
            "x+": device((x + 1) % 4, y, z, c),
            "x-": device((x + 3) % 4, y, z, c),
            "s": device(x, y, z, 1 - c),
        }
        t, s = lax.axis_index("tm"), lax.axis_index("stream")
        self.after = [((t + k) % 32, s) for k in (1, 2)]
        self.before = [((t + 32 - k) % 32, s) for k in (1, 2)]

    def ref(self, kind, part, row, d, core=None, own=False):
        even, odd, size = SPANS[kind][part]
        start = even if even == odd else even + (odd - even) * self.xp
        if kind == "U" and even != odd:
            start = pl.multiple_of(start, 16)
        if own:
            return self.src[kind].at[pl.ds(start, size)]
        yl, zz = (self.y + row) % 2, (self.z + d + 8) % 8
        core = self.c if core is None else core
        if kind == "U":
            return self.buf[kind].at[yl, zz, core, pl.ds(start, size)]
        first = pl.multiple_of(32 * (yl * 16 + zz * 2 + core), 32)
        return self.buf[kind].at[pl.ds(start, size), pl.ds(first, 32)]

    def start(self, src, dst, target, recv):
        copy = pltpu.make_async_remote_copy(
            src_ref=src,
            dst_ref=dst,
            send_sem=self.send_sems.at[len(self.sent)],
            recv_sem=self.recv_sems.at[recv],
            device_id=target,
            device_id_type=MESH,
        )
        copy.start()
        self.sent.append(copy)

    def wait(self, ref, recv):
        pltpu.make_async_remote_copy(
            src_ref=ref,
            dst_ref=ref,
            send_sem=self.send_sems.at[0],
            recv_sem=self.recv_sems.at[recv],
            device_id=self.to["s"],
            device_id_type=MESH,
        ).wait_recv()

    def event(self, kind, part, row, d):
        own = row == 0 and d == 0
        if part == "S":
            self.wait(self.ref(kind, "W", row, d, core=1 - self.c), self.number[kind, part, row, d])
        elif not own:
            self.wait(self.ref(kind, part, row, d), self.number[kind, part, row, d])
        self.here.add((kind, part, row, d))
        for to, sent, link in self.sends.get((kind, part, row, d), ()):
            self.start(
                self.ref(kind, sent, row, d, own=own), self.ref(kind, sent, row, d), self.to[link], self.number[to]
            )
        parts = self.joins.get((kind, row, d), ())
        if part in parts and all((kind, q, row, d) in self.here for q in parts):
            whole = self.ref(kind, "W", row, d)
            self.start(whole, whole, self.to["s"], self.number[kind, "S", row, d])

    def barrier(self):
        semaphore = pltpu.get_barrier_semaphore()
        targets = list(self.to.values()) + self.before
        for target in targets:
            pl.semaphore_signal(semaphore, inc=1, device_id=target, device_id_type=MESH)
        pl.semaphore_wait(semaphore, len(targets))

    def finish(self):
        for copy in self.sent:
            copy.wait_send()


PLAN = (
    ("L", "S", 0, 0), ("L", "M", 0, 1), ("L", "M", 1, 0), ("L", "C", 1, 0), ("norm",), ("L", "C", 0, 1),
    ("L", "Oa", 1, 0), ("L", "M", 0, -1), ("L", "M", 1, 1), ("L", "O", 0, 1), ("k",), ("L", "M", 0, 2),
    ("L", "Ob", 1, 0), ("L", "S", 0, 1), ("L", "C", 0, -1), ("v",), ("q",), ("L", "O", 0, -1), ("L", "S", 1, 0),
    ("L", "M", 0, -2), ("L", "C", 0, 2), ("L", "C", 1, 1), ("att", 0, 0), ("L", "O", 1, 1), ("att", 0, 1),
    ("L", "S", 0, -1), ("L", "M", 0, 3), ("L", "M", 1, -1), ("L", "C", 0, -2), ("L", "C", 1, -1), ("L", "O", 0, 2),
    ("L", "S", 1, 1), ("att", 0, 2), ("L", "M", 1, 2), ("L", "O", 0, -2), ("L", "M", 0, -3), ("L", "M", 1, -2),
    ("att", 1, 0), ("L", "S", 0, 2), ("L", "C", 0, 3), ("att", 1, 1), ("L", "S", 0, -2), ("L", "O", 0, 3),
    ("att", 1, 2), ("L", "C", 1, 2), ("L", "C", 0, -3), ("U", "W", 0, 0), ("L", "C", 1, -2), ("L", "O", 1, -1),
    ("L", "O", 0, -3), ("L", "S", 0, 3), ("L", "M", 1, 3), ("att", 2, 0), ("L", "M", 0, 4), ("L", "M", 1, -3),
    ("L", "O", 1, 2), ("L", "O", 1, -2), ("L", "C", 0, 4), ("U", "S", 0, 0), ("att", 2, 1), ("L", "S", 1, -1),
    ("L", "C", 1, 3), ("L", "S", 0, -3), ("att", 2, 2), ("L", "S", 1, 2), ("L", "C", 1, -3), ("L", "O", 1, 3),
    ("L", "S", 1, -2), ("L", "Ob", 0, 4), ("att", 3, 0), ("L", "Oa", 0, 4), ("att", 3, 1), ("U", "M", 0, -1),
    ("L", "S", 1, 3), ("L", "O", 1, -3), ("U", "M", 0, 1), ("L", "S", 0, 4), ("att", 3, 2), ("U", "M", 1, 0),
    ("post",), ("L", "S", 1, -3), ("L", "Ma", 1, 4), ("U", "C", 1, 0), ("L", "Mb", 1, 4), ("ff", 0),
    ("L", "Ca", 1, 4), ("ff", 1), ("U", "C", 0, -1), ("L", "Cb", 1, 4), ("U", "C", 0, 1), ("ff", 2), ("ff", 3),
    ("ff", 4), ("ff", 5), ("U", "O", 0, -1), ("U", "O", 0, 1), ("ff", 6), ("ff", 7), ("U", "M", 1, -1), ("end",),
    ("U", "M", 0, -2), ("U", "M", 1, 1), ("U", "Oa", 1, 0), ("U", "M", 0, 2), ("U", "Ob", 1, 0), ("U", "S", 0, -1),
    ("L", "Oa", 1, 4), ("L", "Ob", 1, 4), ("U", "S", 0, 1), ("U", "S", 1, 0), ("U", "C", 1, 1), ("L", "S", 1, 4),
    ("la", 0), ("lb", 0), ("U", "C", 0, -2), ("U", "C", 1, -1), ("U", "C", 0, 2), ("la", 1), ("U", "O", 1, -1),
    ("lb", 1), ("la", 2), ("U", "O", 1, 1), ("lb", 2), ("la", 3), ("U", "M", 1, 2), ("U", "S", 1, -1), ("lb", 3),
    ("U", "M", 0, -3), ("U", "M", 1, -2), ("U", "M", 0, 3), ("U", "S", 1, 1), ("up", 0, 0), ("up", 0, 1),
    ("U", "O", 0, -2), ("up", -1, 0), ("up", -1, 1), ("U", "O", 0, 2), ("up", 1, 0), ("up", 1, 1), ("ru", 1),
    ("U", "C", 1, -2), ("U", "S", 0, -2), ("U", "C", 0, -3), ("U", "C", 1, 2), ("U", "C", 0, 3), ("U", "S", 0, 2),
    ("U", "O", 1, 2), ("U", "O", 0, -3), ("U", "S", 1, 2), ("U", "M", 1, -3), ("U", "M", 0, 4), ("U", "M", 1, 3),
    ("U", "S", 0, -3), ("U", "O", 0, 3), ("U", "O", 1, -2), ("U", "C", 0, 4), ("U", "S", 0, 3), ("U", "C", 1, 3),
    ("U", "Oa", 0, 4), ("U", "S", 1, -2), ("up", -2, 0), ("U", "C", 1, -3), ("up", -2, 1), ("U", "O", 1, -3),
    ("ru", 0), ("U", "Ma", 1, 4), ("up", 2, 0), ("U", "Mb", 1, 4), ("up", 2, 1), ("ru", 2), ("U", "Ob", 0, 4),
    ("U", "S", 1, -3), ("U", "Ca", 1, 4), ("up", -3, 0), ("U", "O", 1, 3), ("up", -3, 1), ("U", "Cb", 1, 4),
    ("ru", -1), ("U", "S", 0, 4), ("U", "Oa", 1, 4), ("U", "Ob", 1, 4), ("U", "S", 1, 3), ("up", 3, 0), ("up", 3, 1),
    ("ru", 3), ("U", "S", 1, 4), ("up", 4, 0), ("up", 4, 1), ("ru", 4), ("ru", -2), ("ru", -3),
)


def dot(a, b):
    return jnp.dot(a, b, preferred_element_type=F32)


def dot_nt(a, b):
    return lax.dot_general(a, b, (((1,), (1,)), ((), ())), preferred_element_type=F32)


def elu(v):
    return jnp.where(v > 0, v, jnp.exp(jnp.minimum(v, 0.0)) - 1.0)


def layer_norm(v, gain):
    centred = v - jnp.mean(v, axis=-1, keepdims=True)
    variance = jnp.mean(centred * centred, axis=-1, keepdims=True)
    return centred * lax.rsqrt(variance + 1e-05) * gain


def kernel(
    lat, ga, wq, wk, wv, wo, sa, gf, wup, wdn, sf, wl, bl, wu, bu, wc1, b1, wc2, b2, near, far,
    out,
    lbuf, ubuf, xin, vproj, vup, vdn, vc1, vc2, vga, vsa, vgf, vsf, vbl, vbu, vb1, vb2, vnear, vfar,
    normed, turn, qs, ks, vs, mixed, res, acc, cur7, act2, rect, ups, obf,
    send_sems, recv_sems, here_sems, out_sems,
):
    g = Gather(wl, wu, lbuf, ubuf, send_sems, recv_sems)
    t = lax.axis_index("tm")
    here = []

    def bring(src, dst):
        copy = pltpu.make_async_copy(src, dst, here_sems.at[len(here)])
        copy.start()
        here.append(copy)
        return copy

    own_x = bring(lat, xin.at[pl.ds(HALO, FRAMES)])
    in_ga, in_near, in_far = bring(ga, vga), bring(near, vnear), bring(far, vfar)
    g.barrier()
    g.start(lat, xin.at[pl.ds(LEAD, FRAMES)], g.after[0], 0)
    g.start(lat.at[pl.ds(FRAMES - LEAD, LEAD)], xin.at[pl.ds(0, LEAD)], g.after[1], 1)
    g.event("L", "W", 0, 0)
    in_proj = [bring(w, vproj.at[i]) for i, w in enumerate((wk, wv, wq, wo))]
    own_l = bring(wl, g.ref("L", "W", 0, 0))
    own_u = bring(wu, g.ref("U", "W", 0, 0))
    in_up, in_dn = bring(wup, vup), bring(wdn, vdn)
    in_vec = [
        bring(a, b)
        for a, b in ((sa, vsa), (gf, vgf), (sf, vsf), (bl, vbl), (bu, vbu), (b1, vb1), (b2, vb2))
    ]
    in_c1, in_c2 = bring(wc1, vc1), bring(wc2, vc2)

    lane = lax.broadcasted_iota(jnp.int32, (1, 128), 1)
    first, low = lane % 64 < 32, lane < 64
    live_row = lax.broadcasted_iota(jnp.int32, (LIVE, 1), 0)
    real = (live_row >= LEAD) | (t > 0)
    tail = ROWS - LIVE

    def first_norm():
        own_x.wait()
        g.wait(xin.at[pl.ds(LEAD, FRAMES)], 0)
        g.wait(xin.at[pl.ds(0, LEAD)], 1)
        for copy in (in_ga, in_near, in_far):
            copy.wait()
        normed[...] = layer_norm(xin[...].astype(F32), vga[...]).astype(BF16)
        cos_a, sin_a = vfar[0, pl.ds(t, 1), :], vfar[1, pl.ds(t, 1), :]
        cos_b, sin_b = vnear[0], vnear[1]
        turn[0] = cos_a * cos_b - sin_a * sin_b
        sine = sin_a * cos_b + cos_a * sin_b
        turn[1] = jnp.where(first, -sine, sine)

    def rope(v, skip):
        parts = []
        for i in range(4):
            block = v[:, 128 * i : 128 * i + 128]
            other = jnp.where(first, pltpu.roll(block, 96, 1), pltpu.roll(block, 32, 1))
            parts.append(block * turn[0, skip:] + other * turn[1, skip:])
        return jnp.concatenate(parts, axis=1).astype(BF16)

    def keys():
        in_proj[0].wait()
        ks[...] = rope(dot(normed[...], vproj[0]), 0)

    def values():
        in_proj[1].wait()
        vs[...] = dot(normed[...], vproj[1]).astype(BF16)

    def queries():
        in_proj[2].wait()
        qs[...] = rope(dot(normed[tail:], vproj[2]), tail) * BF16(0.125)

    def attention(pair, block):
        lanes = slice(128 * pair, 128 * pair + 128)
        q0, size, k0, width = ((256, 96, 0, 352), (352, 96, 96, 352), (448, 80, 192, 336))[block]
        q_row = q0 + lax.broadcasted_iota(jnp.int32, (size, width), 0)
        k_row = k0 + lax.broadcasted_iota(jnp.int32, (size, width), 1)
        allowed = (k_row <= q_row) & (k_row > q_row - WIN) & (k_row >= HALO - FRAMES * t)
        q = qs[q0 - tail : q0 - tail + size, lanes]
        k, v = ks[k0 : k0 + width, lanes], vs[k0 : k0 + width, lanes]
        halves = []
        for mask in (low, ~low):
            scores = jnp.where(allowed, dot_nt(jnp.where(mask, q, BF16(0)), k), -1e30)
            weights = jnp.exp(scores - jnp.max(scores, axis=-1, keepdims=True))
            weights = jnp.where(allowed, weights, 0.0)
            total = jnp.maximum(jnp.sum(weights, axis=-1, keepdims=True), 0.5)
            halves.append(dot((weights / total).astype(BF16), v))
        mixed[q0 - tail : q0 - tail + size, lanes] = jnp.where(low, *halves).astype(BF16)

    def after_attention():
        in_proj[3].wait()
        for copy in in_vec:
            copy.wait()
        state = xin[tail:, :].astype(F32)
        residual = state + vsa[...] * dot(mixed[...], vproj[3])
        res[...] = residual
        normed[:LIVE] = layer_norm(residual, vgf[...]).astype(BF16)
        in_up.wait()
        in_dn.wait()

    def feed_forward(i):
        cols = slice(256 * i, 256 * i + 256)
        v = dot(normed[:LIVE], vup[:, cols])
        hidden = (0.5 * v * (1.0 + lax.erf(v * (1.0 / math.sqrt(2.0))))).astype(BF16)
        part = dot(hidden, vdn[cols, :])
        acc[...] = part if i == 0 else acc[...] + part

    def layer_end():
        current = (res[...] + vsf[...] * acc[...]).astype(BF16).astype(F32)
        current = jnp.where(real, current, 0.0)
        for m in range(7):
            moved = pltpu.roll(current, 6 - m, 0) if m < 6 else current
            cur7[:, 512 * m : 512 * m + 512] = moved.astype(BF16)

    def taps(rows, which):
        return sum(dot_nt(cur7[:, 512 * m : 512 * m + 512], lbuf[m, rows, :]) for m in which)

    def lift_begin(i):
        if i == 0:
            own_l.wait()
        acc[:, :256] = taps(slice(256 * i, 256 * i + 256), range(4)) + vbl[:, 256 * i : 256 * i + 256]

    def lift_end(i):
        cols = slice(256 * i, 256 * i + 256)
        total = acc[:, :256] + taps(cols, range(4, 7))
        active = jnp.where(real, elu(total), 0.0).astype(BF16)
        act2[:, cols] = active
        act2[:, C0 + 256 * i : C0 + 256 * i + 256] = pltpu.roll(active.astype(F32), 1, 0).astype(BF16)

    def upsample(d, half):
        if (d, half) == (0, 0):
            own_u.wait()
            in_c1.wait()
            in_c2.wait()
        j = (g.z + d + 8) % 8
        cols = slice(256 * half, 256 * half + 256)
        up = dot(act2[:, :C0], ubuf[0, j, half]) + dot(act2[:, C0:], ubuf[1, j, half])
        up = (up + vbu[:, cols]).astype(BF16)
        ups[j, :, cols] = up[LEAD:]
        rectified = jnp.where(real, elu(up.astype(F32)), 0.0)
        rect[j + 2, :, cols] = rectified.astype(BF16)

        @pl.when(j >= 6)
        def _():
            rect[j - 6, :, cols] = pltpu.roll(rectified, 1, 0).astype(BF16)

    leaving = []

    def residual_unit(d):
        j = (g.z + d + 8) % 8
        total = vb1[...]
        for m in range(3):
            total = total + dot(rect[j + m, LEAD:], vc1[:, CH * m : CH * m + CH])
        second = dot(elu(total).astype(BF16), vc2[...])
        obf[j] = (ups[j].astype(F32) + vb2[...] + second).astype(BF16)
        copy = pltpu.make_async_copy(obf.at[j], out.at[j], out_sems.at[len(leaving)])
        copy.start()
        leaving.append(copy)

    steps = dict(
        norm=first_norm, k=keys, v=values, q=queries, att=attention, post=after_attention, ff=feed_forward,
        end=layer_end, la=lift_begin, lb=lift_end, up=upsample, ru=residual_unit,
    )
    for name, *where in PLAN:
        if name in steps:
            steps[name](*where)
        else:
            g.event(name, *where)
    for copy in leaving:
        copy.wait()
    g.finish()


def weave(phases, out, rows):
    for i in range(4):
        lanes = slice(128 * i, 128 * i + 128)
        for j in range(UPS):
            rows[i, pl.ds(j, phases.shape[1], stride=UPS), :] = phases[j, :, lanes].astype(F32)
        out[:, lanes] = rows[i].astype(BF16)


def tables():
    frequency = 10000.0 ** (-np.arange(32, dtype=np.float64) / 32)
    frequency = np.tile(frequency, 4)[None, :]

    def both(frames):
        angles = frames[:, None] * frequency
        return np.stack([np.cos(angles), np.sin(angles)]).astype(np.float32)

    return both(np.arange(ROWS) - float(HALO)), both(np.arange(32) * float(FRAMES))


def body(
    latents, gain_attn, w_query, w_key, w_value, w_out, scale_attn, gain_ffn, w_up, w_down, scale_ffn,
    w_lift, bias_lift, w_upsample, bias_upsample, w_conv_first, bias_first, w_conv_second, bias_second,
):
    near, far = tables()
    operands = (
        latents[0], gain_attn, w_query[0], w_key[0], w_value[0], w_out[0], scale_attn, gain_ffn, w_up[0], w_down[0],
        scale_ffn, jnp.transpose(w_lift, (0, 2, 1)), bias_lift[None], w_upsample, bias_upsample[None], w_conv_first,
        bias_first[None], w_conv_second, bias_second[None], jnp.asarray(near), jnp.asarray(far),
    )
    vmem = pltpu.VMEM
    dma = pltpu.SemaphoreType.DMA
    phases = pl.pallas_call(
        kernel,
        out_shape=jax.ShapeDtypeStruct((UPS, FRAMES, C1), BF16),
        in_specs=[pl.BlockSpec(memory_space=pl.ANY)] * len(operands),
        out_specs=pl.BlockSpec(memory_space=pl.ANY),
        scratch_shapes=[
            vmem((7, C0, D), BF16),
            vmem((2, UPS, 2, C0, C1 // 2), BF16),
            vmem((ROWS, D), BF16),
            vmem((4, D, D), BF16),
            vmem((D, FF), BF16),
            vmem((FF, D), BF16),
            vmem((C1, 3 * CH), BF16),
            vmem((CH, C1), BF16),
            vmem((1, D), F32),
            vmem((1, D), F32),
            vmem((1, D), F32),
            vmem((1, D), F32),
            vmem((1, C0), F32),
            vmem((1, C1), F32),
            vmem((1, CH), F32),
            vmem((1, C1), F32),
            vmem((2, ROWS, 128), F32),
            vmem((2, 32, 128), F32),
            vmem((ROWS, D), BF16),
            vmem((2, ROWS, 128), F32),
            vmem((LIVE, D), BF16),
            vmem((ROWS, D), BF16),
            vmem((ROWS, D), BF16),
            vmem((LIVE, D), BF16),
            vmem((LIVE, D), F32),
            vmem((LIVE, D), F32),
            vmem((LIVE, 7 * D), BF16),
            vmem((LIVE, 2 * C0), BF16),
            vmem((UPS + 2, LIVE, C1), BF16),
            vmem((UPS, FRAMES, C1), BF16),
            vmem((UPS, FRAMES, C1), BF16),
            dma((140,)),
            dma((140,)),
            dma((24,)),
            dma((8,)),
        ],
        compiler_params=pltpu.CompilerParams(collective_id=0, has_side_effects=True, vmem_limit_bytes=60 * 2**20),
        cost_estimate=pl.CostEstimate(flops=11 * 10**9, bytes_accessed=36 * 10**6, transcendentals=4 * 10**6),
    )(*operands)
    block = 64
    result = pl.pallas_call(
        weave,
        out_shape=jax.ShapeDtypeStruct((FRAMES * UPS, C1), BF16),
        grid=(FRAMES // block,),
        in_specs=[pl.BlockSpec((UPS, block, C1), lambda i: (0, i, 0))],
        out_specs=pl.BlockSpec((UPS * block, C1), lambda i: (i, 0)),
        scratch_shapes=[vmem((4, UPS * block, 128), F32)],
    )(phases)
    return result[None]


def solution(mesh):
    whole = P()
    placed = [whole] * 19
    placed[0] = P("stream", "tm", None)
    placed[11] = P(None, None, "tm")
    placed[13] = P(None, "tm")
    return jax.shard_map(
        body, mesh=mesh, in_specs=tuple(placed), out_specs=P("stream", "tm", None), check_vma=False
    )
```

```python
import math

import jax
import jax.numpy as jnp
import numpy as np
from jax import lax
from jax.experimental import pallas as pl
from jax.experimental.pallas import tpu as pltpu
from jax.sharding import PartitionSpec as P

MESH = pl.DeviceIdType.MESH
BF16, F32 = jnp.bfloat16, jnp.float32
WIN, UPS = 250, 8
FRAMES, D, FF, C0, C1, CH = 256, 512, 2048, 1024, 512, 256
HALO = 272
ROWS = HALO + FRAMES
LIVE = 272
LEAD = LIVE - FRAMES


def coords():
    t = lax.axis_index("tm")
    s = lax.axis_index("stream")
    return s % 4, (s // 4) * 2 + t // 16, (t // 2) % 8, t % 2


def device(x, y, z, c):
    return ((y % 2) * 16 + z * 2 + c, (y // 2) * 4 + x)


SPANS = {
    "L": {
        "W": (0, 0, 7), "P": (0, 2, 5), "C": (2, 2, 3), "Ca": (2, 2, 2), "Cb": (4, 4, 1), "M": (0, 5, 2),
        "Ma": (0, 5, 1), "Mb": (1, 6, 1), "O": (5, 0, 2), "Oa": (5, 0, 1), "Ob": (6, 1, 1),
    },
    "U": {
        "W": (0, 0, 1024), "P": (0, 336, 688), "C": (336, 336, 352), "Ca": (336, 336, 176), "Cb": (512, 512, 176),
        "M": (0, 688, 336), "Ma": (0, 688, 176), "Mb": (176, 864, 160), "O": (688, 0, 336), "Oa": (688, 0, 176),
        "Ob": (864, 176, 160),
    },
}
FROM_CORE = {"S": "W", "SP": "P", "SO": "O"}
NEAR = (-1, 1, -2, 2, -3, 3)
SPLIT_CORE = {"L": False, "U": True}


def routes():
    sends, joins = {}, []
    for kind in "LU":
        split = SPLIT_CORE[kind]

        def add(part, row, d, *items):
            got = sends.setdefault((kind, part, row, d), [])
            for name, to_row, to_d, sent, link in items:
                got.append(((kind, name, to_row, to_d), sent, link))

        def join(row, d, p_parts, o_parts):
            if split:
                joins.append((kind, row, d, p_parts, "SP"))
                joins.append((kind, row, d, o_parts, "SO"))
            else:
                joins.append((kind, row, d, p_parts + o_parts, "S"))

        for p in "MC":
            add(p, 0, 0, (p, 0, -1, p, "z+"), (p, 0, 1, p, "z-"), (p, 1, 0, p, "y+" if p == "M" else "y-"))
        add("C", 0, 0, ("S", 0, 0, "W", "s"))
        add("M", 1, 0, ("Oa", 1, 0, "Ma", "x+"), ("Ob", 1, 0, "Mb", "x-"))
        join(1, 0, ("M", "C"), ("Oa", "Ob"))
        for d in NEAR:
            up, swap = d < 0, d in (-1, 2, -3)
            for p in "MC":
                if abs(d) < 3:
                    add(p, 0, d, (p, 0, d - 1 if up else d + 1, p, "z+" if up else "z-"))
                else:
                    half = p + ("a" if up else "b")
                    add(p, 0, d, (half, 0, 4, half, "z+" if up else "z-"))
                add(p, 0, d, (p, 1, d, p, "y+" if swap == (p == "M") else "y-"))
            for row in (0, 1):
                add("M", row, d, ("O", row, d, "M", "x+" if swap == (row == 0) else "x-"))
                join(row, d, ("M", "C"), ("O",))
        for p, y in (("Ma", "y+"), ("Mb", "y-"), ("Ca", "y+"), ("Cb", "y-")):
            add(p, 0, 4, (p, 1, 4, p, y))
        for row in (0, 1):
            add("Ma", row, 4, ("Oa", row, 4, "Ma", "x+"))
            add("Mb", row, 4, ("Ob", row, 4, "Mb", "x-"))
            join(row, 4, ("Ma", "Mb", "Ca", "Cb"), ("Oa", "Ob"))
    return sends, joins


class Gather:
    def __init__(self, wl, wu, lbuf, ubuf, send_sems, recv_sems):
        self.x, self.y, self.z, self.c = x, y, z, c = coords()
        self.xp = self.x % 2
        self.src = {"L": wl, "U": wu}
        self.buf = {"L": lbuf, "U": ubuf}
        self.send_sems, self.recv_sems = send_sems, recv_sems
        self.sent = []
        self.sends, self.joins = routes()
        arrivals = [to for sends in self.sends.values() for to, _, _ in sends]
        arrivals += [(kind, name, row, d) for kind, row, d, _, name in self.joins]
        self.number = {to: i + 2 for i, to in enumerate(arrivals)}
        self.here = set()
        self.to = {
            "z+": device(x, y, (z + 1) % 8, c),
            "z-": device(x, y, (z + 7) % 8, c),
            "y+": device(x, (y + 1) % 4, z, c),
            "y-": device(x, (y + 3) % 4, z, c),
            "x+": device((x + 1) % 4, y, z, c),
            "x-": device((x + 3) % 4, y, z, c),
            "s": device(x, y, z, 1 - c),
        }
        t, s = lax.axis_index("tm"), lax.axis_index("stream")
        self.after = [((t + k) % 32, s) for k in (1, 2)]
        self.before = [((t + 32 - k) % 32, s) for k in (1, 2)]

    def ref(self, kind, part, row, d, core=None, own=False):
        even, odd, size = SPANS[kind][part]
        start = even if even == odd else even + (odd - even) * self.xp
        if kind == "U" and even != odd:
            start = pl.multiple_of(start, 16)
        if own:
            return self.src[kind].at[pl.ds(start, size)]
        yl, zz = (self.y + row) % 2, (self.z + d + 8) % 8
        core = self.c if core is None else core
        if kind == "U":
            return self.buf[kind].at[yl, zz, core, pl.ds(start, size)]
        first = pl.multiple_of(32 * (yl * 16 + zz * 2 + core), 32)
        return self.buf[kind].at[pl.ds(start, size), pl.ds(first, 32)]

    def start(self, src, dst, target, recv):
        copy = pltpu.make_async_remote_copy(
            src_ref=src,
            dst_ref=dst,
            send_sem=self.send_sems.at[len(self.sent)],
            recv_sem=self.recv_sems.at[recv],
            device_id=target,
            device_id_type=MESH,
        )
        copy.start()
        self.sent.append(copy)

    def wait(self, ref, recv):
        pltpu.make_async_remote_copy(
            src_ref=ref,
            dst_ref=ref,
            send_sem=self.send_sems.at[0],
            recv_sem=self.recv_sems.at[recv],
            device_id=self.to["s"],
            device_id_type=MESH,
        ).wait_recv()

    def event(self, kind, part, row, d):
        own = row == 0 and d == 0
        if part in FROM_CORE:
            self.wait(self.ref(kind, FROM_CORE[part], row, d, core=1 - self.c), self.number[kind, part, row, d])
        elif not own:
            self.wait(self.ref(kind, part, row, d), self.number[kind, part, row, d])
        self.here.add((kind, part, row, d))
        for to, sent, link in self.sends.get((kind, part, row, d), ()):
            self.start(
                self.ref(kind, sent, row, d, own=own), self.ref(kind, sent, row, d), self.to[link], self.number[to]
            )
        for of_kind, of_row, of_d, parts, name in self.joins:
            if (of_kind, of_row, of_d) == (kind, row, d) and part in parts:
                if all((kind, p, row, d) in self.here for p in parts):
                    whole = self.ref(kind, FROM_CORE[name], row, d)
                    self.start(whole, whole, self.to["s"], self.number[kind, name, row, d])

    def barrier(self):
        semaphore = pltpu.get_barrier_semaphore()
        targets = list(self.to.values()) + self.before
        for target in targets:
            pl.semaphore_signal(semaphore, inc=1, device_id=target, device_id_type=MESH)
        pl.semaphore_wait(semaphore, len(targets))

    def finish(self):
        for copy in self.sent:
            copy.wait_send()


PLAN = (
    ("L", "S", 0, 0), ("L", "M", 0, 1), ("L", "M", 1, 0), ("L", "C", 1, 0), ("norm",), ("L", "C", 0, 1),
    ("L", "M", 0, -1), ("k",), ("L", "Oa", 1, 0), ("L", "M", 0, 2), ("L", "M", 1, 1), ("L", "O", 0, 1), ("v",),
    ("L", "Ob", 1, 0), ("L", "C", 0, -1), ("U", "M", 0, 0), ("q",), ("L", "S", 0, 1), ("att", 0, 0), ("L", "S", 1, 0),
    ("L", "M", 0, -2), ("L", "O", 0, -1), ("att", 0, 1), ("L", "C", 0, 2), ("L", "C", 1, 1), ("att", 0, 2),
    ("L", "O", 0, 2), ("L", "S", 0, -1), ("L", "M", 0, 3), ("L", "M", 1, -1), ("att", 1, 0), ("L", "O", 1, 1),
    ("L", "C", 0, -2), ("L", "C", 1, -1), ("att", 1, 1), ("L", "M", 1, 2), ("L", "S", 0, 2), ("L", "O", 0, -2),
    ("att", 1, 2), ("L", "M", 1, -2), ("L", "S", 1, 1), ("att", 2, 0), ("L", "S", 0, -2), ("U", "M", 0, 1),
    ("L", "O", 0, 3), ("att", 2, 1), ("L", "C", 1, 2), ("U", "M", 0, -1), ("att", 2, 2), ("U", "M", 1, 0),
    ("L", "O", 1, -1), ("L", "C", 0, 3), ("L", "M", 1, 3), ("L", "M", 0, -3), ("att", 3, 0), ("L", "Mb", 0, 4),
    ("L", "O", 1, 2), ("L", "O", 1, -2), ("L", "C", 1, -2), ("U", "C", 0, 0), ("L", "S", 1, -1), ("att", 3, 1),
    ("L", "S", 0, 3), ("L", "C", 0, -3), ("att", 3, 2), ("L", "S", 1, 2), ("L", "S", 1, -2), ("post",),
    ("U", "S", 0, 0), ("U", "M", 1, 1), ("U", "M", 0, 2), ("ff", 0), ("U", "O", 0, 1), ("L", "Mb", 1, 4),
    ("L", "Cb", 0, 4), ("U", "M", 1, -1), ("U", "O", 0, -1), ("ff", 1), ("ff", 2), ("U", "M", 0, -2),
    ("U", "SO", 0, 1), ("U", "Ob", 1, 0), ("ff", 3), ("U", "SO", 0, -1), ("L", "Ma", 0, 4), ("L", "Ob", 0, 4),
    ("U", "Oa", 1, 0), ("ff", 4), ("L", "C", 1, 3), ("ff", 5), ("ff", 6), ("L", "Ob", 1, 4), ("U", "SO", 1, 0),
    ("L", "O", 1, 3), ("L", "M", 1, -3), ("U", "C", 1, 0), ("U", "C", 0, 1), ("ff", 7), ("end",), ("L", "O", 0, -3),
    ("L", "S", 1, 3), ("U", "C", 0, -1), ("U", "SP", 1, 0), ("L", "C", 1, -3), ("U", "SP", 0, 1), ("L", "Cb", 1, 4),
    ("L", "S", 0, -3), ("L", "Ca", 0, 4), ("U", "O", 1, -1), ("U", "M", 1, 2), ("U", "SP", 0, -1), ("U", "M", 0, 3),
    ("L", "Ma", 1, 4), ("U", "SO", 1, -1), ("U", "O", 1, 1), ("U", "SO", 1, 1), ("U", "M", 1, -2), ("U", "M", 0, -3),
    ("U", "O", 0, -2), ("U", "C", 0, 2), ("U", "C", 1, 1), ("U", "SO", 0, -2), ("L", "O", 1, -3), ("U", "O", 0, 2),
    ("U", "SP", 0, 2), ("L", "Oa", 0, 4), ("U", "Mb", 0, 4), ("L", "Ca", 1, 4), ("U", "SP", 1, 1), ("L", "Oa", 1, 4),
    ("L", "S", 1, -3), ("U", "C", 1, -1), ("U", "SO", 0, 2), ("U", "C", 0, -2), ("L", "S", 0, 4), ("L", "S", 1, 4),
    ("lift", 0), ("U", "O", 1, 2), ("U", "SP", 1, -1), ("lift", 1), ("U", "Ma", 0, 4), ("U", "SP", 0, -2),
    ("lift", 2), ("U", "M", 1, -3), ("U", "SO", 1, 2), ("U", "O", 1, -2), ("U", "C", 0, 3), ("U", "M", 1, 3),
    ("lift", 3), ("up", 0, ()), ("U", "SO", 1, -2), ("U", "O", 0, 3), ("U", "SP", 0, 3), ("up", -1, ()),
    ("U", "C", 0, -3), ("U", "C", 1, -2), ("U", "SO", 0, 3), ("U", "O", 0, -3), ("U", "Ob", 0, 4), ("up", 1, ()),
    ("U", "C", 1, 2), ("U", "Cb", 0, 4), ("U", "SP", 0, -3), ("U", "Ma", 1, 4), ("U", "Oa", 0, 4), ("U", "SP", 1, -2),
    ("up", -2, (1,)), ("U", "Mb", 1, 4), ("U", "SO", 0, -3), ("U", "SP", 1, 2), ("U", "SO", 0, 4), ("U", "O", 1, -3),
    ("up", 2, (0,)), ("U", "Ca", 0, 4), ("U", "SO", 1, -3), ("U", "C", 1, 3), ("U", "O", 1, 3), ("U", "C", 1, -3),
    ("U", "SP", 0, 4), ("U", "Oa", 1, 4), ("U", "SP", 1, 3), ("U", "Ob", 1, 4), ("U", "SO", 1, 3), ("U", "Cb", 1, 4),
    ("U", "SP", 1, -3), ("up", -3, (2,)), ("U", "SO", 1, 4), ("U", "Ca", 1, 4), ("up", 3, (-1,)), ("U", "SP", 1, 4),
    ("early", 3), ("row",), ("up", 4, ()), ("last",),
)


def dot(a, b):
    return jnp.dot(a, b, preferred_element_type=F32)


def dot_nt(a, b):
    return lax.dot_general(a, b, (((1,), (1,)), ((), ())), preferred_element_type=F32)


def elu(v):
    return jnp.where(v > 0, v, jnp.exp(jnp.minimum(v, 0.0)) - 1.0)


def layer_norm(v, gain):
    centred = v - jnp.mean(v, axis=-1, keepdims=True)
    variance = jnp.mean(centred * centred, axis=-1, keepdims=True)
    return centred * lax.rsqrt(variance + 1e-05) * gain


def kernel(
    lat, ga, wq, wk, wv, wo, sa, gf, wup, wdn, sf, wl, bl, wu, bu, wc1, b1, wc2, b2, near, far,
    out,
    lbuf, ubuf, xin, vproj, vup, vdn, vc1, vc2, vga, vsa, vgf, vsf, vbl, vbu, vb1, vb2, vnear, vfar,
    normed, turn, qs, ks, vs, mixed, res, acc, cur7, act2, rect, part, ups, obf,
    send_sems, recv_sems, here_sems, out_sems,
):
    g = Gather(wl, wu, lbuf, ubuf, send_sems, recv_sems)
    t = lax.axis_index("tm")
    here = []

    def bring(src, dst):
        copy = pltpu.make_async_copy(src, dst, here_sems.at[len(here)])
        copy.start()
        here.append(copy)
        return copy

    own_x = bring(lat, xin.at[pl.ds(HALO, FRAMES)])
    in_ga, in_near, in_far = bring(ga, vga), bring(near, vnear), bring(far, vfar)
    g.barrier()
    g.start(lat, xin.at[pl.ds(LEAD, FRAMES)], g.after[0], 0)
    g.start(lat.at[pl.ds(FRAMES - LEAD, LEAD)], xin.at[pl.ds(0, LEAD)], g.after[1], 1)
    g.event("L", "M", 0, 0)
    g.event("L", "C", 0, 0)
    in_proj = [bring(w, vproj.at[i]) for i, w in enumerate((wk, wv, wq, wo))]
    own_l = bring(wl, g.ref("L", "W", 0, 0))
    own_u = bring(wu, g.ref("U", "W", 0, 0))
    in_up, in_dn = bring(wup, vup), bring(wdn, vdn)
    in_vec = [
        bring(a, b)
        for a, b in ((sa, vsa), (gf, vgf), (sf, vsf), (bl, vbl), (bu, vbu), (b1, vb1), (b2, vb2))
    ]
    in_c1, in_c2 = bring(wc1, vc1), bring(wc2, vc2)

    lane = lax.broadcasted_iota(jnp.int32, (1, 128), 1)
    first, low = lane % 64 < 32, lane < 64
    live_row = lax.broadcasted_iota(jnp.int32, (LIVE, 1), 0)
    real = (live_row >= LEAD) | (t > 0)
    tail = ROWS - LIVE

    def first_norm():
        own_x.wait()
        g.wait(xin.at[pl.ds(LEAD, FRAMES)], 0)
        g.wait(xin.at[pl.ds(0, LEAD)], 1)
        for copy in (in_ga, in_near, in_far):
            copy.wait()
        normed[...] = layer_norm(xin[...].astype(F32), vga[...]).astype(BF16)
        cos_a, sin_a = vfar[0, pl.ds(t, 1), :], vfar[1, pl.ds(t, 1), :]
        cos_b, sin_b = vnear[0], vnear[1]
        turn[0] = cos_a * cos_b - sin_a * sin_b
        sine = sin_a * cos_b + cos_a * sin_b
        turn[1] = jnp.where(first, -sine, sine)

    def rope(v, skip):
        parts = []
        for i in range(4):
            block = v[:, 128 * i : 128 * i + 128]
            other = jnp.where(first, pltpu.roll(block, 96, 1), pltpu.roll(block, 32, 1))
            parts.append(block * turn[0, skip:] + other * turn[1, skip:])
        return jnp.concatenate(parts, axis=1).astype(BF16)

    def keys():
        in_proj[0].wait()
        ks[...] = rope(dot(normed[...], vproj[0]), 0)

    def values():
        in_proj[1].wait()
        vs[...] = dot(normed[...], vproj[1]).astype(BF16)

    def queries():
        in_proj[2].wait()
        qs[...] = rope(dot(normed[tail:], vproj[2]), tail) * BF16(0.125)

    def attention(pair, block):
        lanes = slice(128 * pair, 128 * pair + 128)
        q0, size, k0, width = ((256, 96, 0, 352), (352, 96, 96, 352), (448, 80, 192, 336))[block]
        q_row = q0 + lax.broadcasted_iota(jnp.int32, (size, width), 0)
        k_row = k0 + lax.broadcasted_iota(jnp.int32, (size, width), 1)
        allowed = (k_row <= q_row) & (k_row > q_row - WIN) & (k_row >= HALO - FRAMES * t)
        q = qs[q0 - tail : q0 - tail + size, lanes]
        k, v = ks[k0 : k0 + width, lanes], vs[k0 : k0 + width, lanes]
        halves = []
        for mask in (low, ~low):
            scores = jnp.where(allowed, dot_nt(jnp.where(mask, q, BF16(0)), k), -1e30)
            weights = jnp.exp(scores - jnp.max(scores, axis=-1, keepdims=True))
            weights = jnp.where(allowed, weights, 0.0)
            total = jnp.maximum(jnp.sum(weights, axis=-1, keepdims=True), 0.5)
            halves.append(dot((weights / total).astype(BF16), v))
        mixed[q0 - tail : q0 - tail + size, lanes] = jnp.where(low, *halves).astype(BF16)

    def after_attention():
        in_proj[3].wait()
        for copy in in_vec:
            copy.wait()
        state = xin[tail:, :].astype(F32)
        residual = state + vsa[...] * dot(mixed[...], vproj[3])
        res[...] = residual
        normed[:LIVE] = layer_norm(residual, vgf[...]).astype(BF16)
        in_up.wait()
        in_dn.wait()

    def feed_forward(i):
        cols = slice(256 * i, 256 * i + 256)
        v = dot(normed[:LIVE], vup[:, cols])
        hidden = (0.5 * v * (1.0 + lax.erf(v * (1.0 / math.sqrt(2.0))))).astype(BF16)
        more = dot(hidden, vdn[cols, :])
        acc[...] = more if i == 0 else acc[...] + more

    def layer_end():
        current = (res[...] + vsf[...] * acc[...]).astype(BF16).astype(F32)
        current = jnp.where(real, current, 0.0)
        for m in range(7):
            moved = pltpu.roll(current, 6 - m, 0) if m < 6 else current
            cur7[:, 512 * m : 512 * m + 512] = moved.astype(BF16)

    def lift(i):
        if i == 0:
            own_l.wait()
        cols = slice(256 * i, 256 * i + 256)
        total = sum(dot_nt(cur7[:, 512 * m : 512 * m + 512], lbuf[m, cols, :]) for m in range(7)) + vbl[:, cols]
        active = jnp.where(real, elu(total), 0.0).astype(BF16)
        act2[:, cols] = active
        act2[:, C0 + 256 * i : C0 + 256 * i + 256] = pltpu.roll(active.astype(F32), 1, 0).astype(BF16)

    def phase(d):
        return (g.z + d + 8) % 8

    def tap(row, j, half):
        yl = (g.y + row) % 2
        return dot(act2[:, pl.ds(pl.multiple_of(C0 * yl, C0), C0)], ubuf[yl, j, half])

    def upsample(d, units):
        if d == 0:
            own_u.wait()
            in_c1.wait()
            in_c2.wait()
        for u in units:
            residual_unit(u)
        j = phase(d)
        for half in range(2):
            cols = slice(256 * half, 256 * half + 256)
            if d == 4:
                up = acc[:, cols] + tap(1, j, half)
            else:
                up = dot(act2[:, :C0], ubuf[0, j, half]) + dot(act2[:, C0:], ubuf[1, j, half])
            up = (up + vbu[:, cols]).astype(BF16)
            ups[j, :, cols] = up[LEAD:]
            rectified = elu(up.astype(F32)).astype(BF16)
            rect[j + 2, :LEAD, cols] = jnp.where(t > 0, rectified[:LEAD], BF16(0))
            rect[j + 2, LEAD:, cols] = rectified[LEAD:]

        @pl.when(j >= 6)
        def _():
            rect[j - 6] = pltpu.roll(rect[j + 2].astype(F32), 1, 0).astype(BF16)

    leaving = []
    last_tap = {4: 2, -3: 1, -2: 0}

    def conv(j, m):
        return dot(rect[j + m, LEAD:], vc1[:, CH * m : CH * m + CH])

    def last_begin(*units):
        for u in units:
            residual_unit(u)
        for u, last in last_tap.items():
            one, two = (m for m in range(3) if m != last)
            part[last] = vb1[...] + conv(phase(u), one) + conv(phase(u), two)

    def last_row():
        for half in range(2):
            acc[:, 256 * half : 256 * half + 256] = tap(0, phase(4), half)

    def residual_unit(d):
        j = phase(d)
        if d in last_tap:
            total = part[last_tap[d]] + conv(j, last_tap[d])
        else:
            total = vb1[...] + conv(j, 0) + conv(j, 1) + conv(j, 2)
        second = dot(elu(total).astype(BF16), vc2[...])
        obf[j] = (ups[j].astype(F32) + vb2[...] + second).astype(BF16)
        copy = pltpu.make_async_copy(obf.at[j], out.at[j], out_sems.at[len(leaving)])
        copy.start()
        leaving.append(copy)

    def last_units():
        for d in last_tap:
            residual_unit(d)

    steps = dict(
        norm=first_norm, k=keys, v=values, q=queries, att=attention, post=after_attention, ff=feed_forward,
        end=layer_end, lift=lift, up=upsample, early=last_begin, row=last_row, last=last_units,
    )
    for name, *where in PLAN:
        if name in steps:
            steps[name](*where)
        else:
            g.event(name, *where)
    for copy in leaving:
        copy.wait()
    g.finish()


def weave(phases, out, rows):
    for i in range(4):
        lanes = slice(128 * i, 128 * i + 128)
        for j in range(UPS):
            rows[i, pl.ds(j, phases.shape[1], stride=UPS), :] = phases[j, :, lanes].astype(F32)
        out[:, lanes] = rows[i].astype(BF16)


def tables():
    frequency = 10000.0 ** (-np.arange(32, dtype=np.float64) / 32)
    frequency = np.tile(frequency, 4)[None, :]

    def both(frames):
        angles = frames[:, None] * frequency
        return np.stack([np.cos(angles), np.sin(angles)]).astype(np.float32)

    return both(np.arange(ROWS) - float(HALO)), both(np.arange(32) * float(FRAMES))


def body(
    latents, gain_attn, w_query, w_key, w_value, w_out, scale_attn, gain_ffn, w_up, w_down, scale_ffn,
    w_lift, bias_lift, w_upsample, bias_upsample, w_conv_first, bias_first, w_conv_second, bias_second,
):
    near, far = tables()
    operands = (
        latents[0], gain_attn, w_query[0], w_key[0], w_value[0], w_out[0], scale_attn, gain_ffn, w_up[0], w_down[0],
        scale_ffn, jnp.transpose(w_lift, (0, 2, 1)), bias_lift[None], w_upsample, bias_upsample[None], w_conv_first,
        bias_first[None], w_conv_second, bias_second[None], jnp.asarray(near), jnp.asarray(far),
    )
    vmem = pltpu.VMEM
    dma = pltpu.SemaphoreType.DMA
    phases = pl.pallas_call(
        kernel,
        out_shape=jax.ShapeDtypeStruct((UPS, FRAMES, C1), BF16),
        in_specs=[pl.BlockSpec(memory_space=pl.ANY)] * len(operands),
        out_specs=pl.BlockSpec(memory_space=pl.ANY),
        scratch_shapes=[
            vmem((7, C0, D), BF16),
            vmem((2, UPS, 2, C0, C1 // 2), BF16),
            vmem((ROWS, D), BF16),
            vmem((4, D, D), BF16),
            vmem((D, FF), BF16),
            vmem((FF, D), BF16),
            vmem((C1, 3 * CH), BF16),
            vmem((CH, C1), BF16),
            vmem((1, D), F32),
            vmem((1, D), F32),
            vmem((1, D), F32),
            vmem((1, D), F32),
            vmem((1, C0), F32),
            vmem((1, C1), F32),
            vmem((1, CH), F32),
            vmem((1, C1), F32),
            vmem((2, ROWS, 128), F32),
            vmem((2, 32, 128), F32),
            vmem((ROWS, D), BF16),
            vmem((2, ROWS, 128), F32),
            vmem((LIVE, D), BF16),
            vmem((ROWS, D), BF16),
            vmem((ROWS, D), BF16),
            vmem((LIVE, D), BF16),
            vmem((LIVE, D), F32),
            vmem((LIVE, D), F32),
            vmem((LIVE, 7 * D), BF16),
            vmem((LIVE, 2 * C0), BF16),
            vmem((UPS + 2, LIVE, C1), BF16),
            vmem((3, FRAMES, CH), F32),
            vmem((UPS, FRAMES, C1), BF16),
            vmem((UPS, FRAMES, C1), BF16),
            dma((172,)),
            dma((172,)),
            dma((24,)),
            dma((8,)),
        ],
        compiler_params=pltpu.CompilerParams(collective_id=0, has_side_effects=True, vmem_limit_bytes=60 * 2**20),
        cost_estimate=pl.CostEstimate(flops=11 * 10**9, bytes_accessed=36 * 10**6, transcendentals=4 * 10**6),
    )(*operands)
    block = 128
    result = pl.pallas_call(
        weave,
        out_shape=jax.ShapeDtypeStruct((FRAMES * UPS, C1), BF16),
        grid=(FRAMES // block,),
        in_specs=[pl.BlockSpec((UPS, block, C1), lambda i: (0, i, 0))],
        out_specs=pl.BlockSpec((UPS * block, C1), lambda i: (i, 0)),
        scratch_shapes=[vmem((4, UPS * block, 128), F32)],
    )(phases)
    return result[None]


def solution(mesh):
    whole = P()
    placed = [whole] * 19
    placed[0] = P("stream", "tm", None)
    placed[11] = P(None, None, "tm")
    placed[13] = P(None, "tm")
    return jax.shard_map(
        body, mesh=mesh, in_specs=tuple(placed), out_specs=P("stream", "tm", None), check_vma=False
    )
```

```python
import math

import jax
import jax.numpy as jnp
import numpy as np
from jax import lax
from jax.experimental import pallas as pl
from jax.experimental.pallas import tpu as pltpu
from jax.sharding import PartitionSpec as P

MESH = pl.DeviceIdType.MESH
BF16, F32 = jnp.bfloat16, jnp.float32
WIN, UPS = 250, 8
FRAMES, D, FF, C0, C1, CH = 256, 512, 2048, 1024, 512, 256
HALO = 272
ROWS = HALO + FRAMES
LIVE = 272
LEAD = LIVE - FRAMES


def coords():
    t = lax.axis_index("tm")
    s = lax.axis_index("stream")
    return s % 4, (s // 4) * 2 + t // 16, (t // 2) % 8, t % 2


def device(x, y, z, c):
    return ((y % 2) * 16 + z * 2 + c, (y // 2) * 4 + x)


SPANS = {
    "L": {
        "W": (0, 0, 7), "P": (0, 2, 5), "C": (2, 2, 3), "Ca": (2, 2, 2), "Cb": (4, 4, 1), "M": (0, 5, 2),
        "Ma": (0, 5, 1), "Mb": (1, 6, 1), "O": (5, 0, 2), "Oa": (5, 0, 1), "Ob": (6, 1, 1),
    },
    "U": {
        "W": (0, 0, 1024), "P": (0, 336, 688), "C": (336, 336, 352), "Ca": (336, 336, 176), "Cb": (512, 512, 176),
        "M": (0, 688, 336), "Ma": (0, 688, 176), "Mb": (176, 864, 160), "O": (688, 0, 336), "Oa": (688, 0, 176),
        "Ob": (864, 176, 160),
    },
}
FROM_CORE = {"S": "W", "SP": "P", "SO": "O"}
NEAR = (-1, 1, -2, 2, -3, 3)
SPLIT_CORE = {"L": False, "U": True}


def routes():
    sends, joins = {}, []
    for kind in "LU":
        split = SPLIT_CORE[kind]

        def add(part, row, d, *items):
            got = sends.setdefault((kind, part, row, d), [])
            for name, to_row, to_d, sent, link in items:
                got.append(((kind, name, to_row, to_d), sent, link))

        def join(row, d, p_parts, o_parts):
            if split:
                joins.append((kind, row, d, p_parts, "SP"))
                joins.append((kind, row, d, o_parts, "SO"))
            else:
                joins.append((kind, row, d, p_parts + o_parts, "S"))

        for p in "MC":
            add(p, 0, 0, (p, 0, -1, p, "z+"), (p, 0, 1, p, "z-"), (p, 1, 0, p, "y+" if p == "M" else "y-"))
        add("C", 0, 0, ("S", 0, 0, "W", "s"))
        add("M", 1, 0, ("Oa", 1, 0, "Ma", "x+"), ("Ob", 1, 0, "Mb", "x-"))
        join(1, 0, ("M", "C"), ("Oa", "Ob"))
        for d in NEAR:
            up, swap = d < 0, d in (-1, 2, -3)
            for p in "MC":
                if abs(d) < 3:
                    add(p, 0, d, (p, 0, d - 1 if up else d + 1, p, "z+" if up else "z-"))
                else:
                    half = p + ("a" if up else "b")
                    add(p, 0, d, (half, 0, 4, half, "z+" if up else "z-"))
                add(p, 0, d, (p, 1, d, p, "y+" if swap == (p == "M") else "y-"))
            for row in (0, 1):
                add("M", row, d, ("O", row, d, "M", "x+" if swap == (row == 0) else "x-"))
                join(row, d, ("M", "C"), ("O",))
        for p, y in (("Ma", "y+"), ("Mb", "y-"), ("Ca", "y+"), ("Cb", "y-")):
            add(p, 0, 4, (p, 1, 4, p, y))
        for row in (0, 1):
            add("Ma", row, 4, ("Oa", row, 4, "Ma", "x+"))
            add("Mb", row, 4, ("Ob", row, 4, "Mb", "x-"))
            join(row, 4, ("Ma", "Mb", "Ca", "Cb"), ("Oa", "Ob"))
    return sends, joins


class Gather:
    def __init__(self, wl, wu, lbuf, ubuf, send_sems, recv_sems):
        self.x, self.y, self.z, self.c = x, y, z, c = coords()
        self.xp = self.x % 2
        self.src = {"L": wl, "U": wu}
        self.buf = {"L": lbuf, "U": ubuf}
        self.send_sems, self.recv_sems = send_sems, recv_sems
        self.sent = []
        self.sends, self.joins = routes()
        arrivals = [to for sends in self.sends.values() for to, _, _ in sends]
        arrivals += [(kind, name, row, d) for kind, row, d, _, name in self.joins]
        self.number = {to: i + 2 for i, to in enumerate(arrivals)}
        self.here = set()
        self.to = {
            "z+": device(x, y, (z + 1) % 8, c),
            "z-": device(x, y, (z + 7) % 8, c),
            "y+": device(x, (y + 1) % 4, z, c),
            "y-": device(x, (y + 3) % 4, z, c),
            "x+": device((x + 1) % 4, y, z, c),
            "x-": device((x + 3) % 4, y, z, c),
            "s": device(x, y, z, 1 - c),
        }
        t, s = lax.axis_index("tm"), lax.axis_index("stream")
        self.after = [((t + k) % 32, s) for k in (1, 2)]
        self.before = [((t + 32 - k) % 32, s) for k in (1, 2)]

    def ref(self, kind, part, row, d, core=None, own=False):
        even, odd, size = SPANS[kind][part]
        start = even if even == odd else even + (odd - even) * self.xp
        if kind == "U" and even != odd:
            start = pl.multiple_of(start, 16)
        if own:
            return self.src[kind].at[pl.ds(start, size)]
        yl, zz = (self.y + row) % 2, (self.z + d + 8) % 8
        core = self.c if core is None else core
        if kind == "U":
            return self.buf[kind].at[yl, zz, core, pl.ds(start, size)]
        first = pl.multiple_of(32 * (yl * 16 + zz * 2 + core), 32)
        return self.buf[kind].at[pl.ds(start, size), pl.ds(first, 32)]

    def start(self, src, dst, target, recv):
        copy = pltpu.make_async_remote_copy(
            src_ref=src,
            dst_ref=dst,
            send_sem=self.send_sems.at[len(self.sent)],
            recv_sem=self.recv_sems.at[recv],
            device_id=target,
            device_id_type=MESH,
        )
        copy.start()
        self.sent.append(copy)

    def wait(self, ref, recv):
        pltpu.make_async_remote_copy(
            src_ref=ref,
            dst_ref=ref,
            send_sem=self.send_sems.at[0],
            recv_sem=self.recv_sems.at[recv],
            device_id=self.to["s"],
            device_id_type=MESH,
        ).wait_recv()

    def event(self, kind, part, row, d):
        own = row == 0 and d == 0
        if part in FROM_CORE:
            self.wait(self.ref(kind, FROM_CORE[part], row, d, core=1 - self.c), self.number[kind, part, row, d])
        elif not own:
            self.wait(self.ref(kind, part, row, d), self.number[kind, part, row, d])
        self.here.add((kind, part, row, d))
        for to, sent, link in self.sends.get((kind, part, row, d), ()):
            self.start(
                self.ref(kind, sent, row, d, own=own), self.ref(kind, sent, row, d), self.to[link], self.number[to]
            )
        for of_kind, of_row, of_d, parts, name in self.joins:
            if (of_kind, of_row, of_d) == (kind, row, d) and part in parts:
                if all((kind, p, row, d) in self.here for p in parts):
                    whole = self.ref(kind, FROM_CORE[name], row, d)
                    self.start(whole, whole, self.to["s"], self.number[kind, name, row, d])

    def barrier(self):
        semaphore = pltpu.get_barrier_semaphore()
        targets = list(self.to.values()) + self.before
        for target in targets:
            pl.semaphore_signal(semaphore, inc=1, device_id=target, device_id_type=MESH)
        pl.semaphore_wait(semaphore, len(targets))

    def finish(self):
        for copy in self.sent:
            copy.wait_send()


PLAN = (
    ("L", "S", 0, 0), ("L", "M", 0, -1), ("L", "M", 0, 1), ("L", "M", 1, 0), ("L", "C", 1, 0), ("L", "C", 0, -1),
    ("U", "M", 0, 0), ("L", "C", 0, 1), ("L", "M", 1, -1), ("L", "O", 0, -1), ("L", "M", 0, 2), ("L", "M", 1, 1),
    ("L", "O", 0, 1), ("L", "Oa", 1, 0), ("L", "Ob", 1, 0), ("L", "S", 0, -1), ("L", "S", 0, 1), ("L", "S", 1, 0),
    ("norm",), ("L", "C", 1, -1), ("L", "O", 1, -1), ("L", "M", 0, -2), ("L", "O", 0, 2), ("k",), ("U", "M", 0, 1),
    ("U", "M", 1, 0), ("L", "S", 1, -1), ("L", "O", 1, 1), ("v",), ("L", "C", 0, -2), ("q",), ("L", "C", 0, 2),
    ("L", "C", 1, 1), ("att", 0, 0), ("L", "M", 1, -2), ("L", "O", 0, -2), ("L", "M", 0, 3), ("L", "M", 1, 2),
    ("att", 0, 1), ("L", "S", 0, 2), ("L", "S", 1, 1), ("att", 0, 2), ("L", "S", 0, -2), ("U", "M", 0, -1),
    ("U", "Oa", 1, 0), ("att", 1, 0), ("L", "C", 1, -2), ("U", "C", 0, 0), ("L", "M", 0, -3), ("att", 1, 1),
    ("U", "M", 1, 1), ("U", "O", 0, 1), ("U", "M", 0, 2), ("L", "O", 1, -2), ("att", 1, 2), ("U", "S", 0, 0),
    ("L", "C", 0, -3), ("att", 2, 0), ("U", "Ob", 1, 0), ("U", "SO", 0, 1), ("L", "C", 1, 2), ("L", "C", 0, 3),
    ("L", "S", 1, -2), ("att", 2, 1), ("L", "Mb", 0, 4), ("L", "O", 0, 3), ("L", "M", 1, 3), ("U", "SO", 1, 0),
    ("att", 2, 2), ("U", "M", 1, -1), ("L", "O", 1, 2), ("U", "O", 0, -1), ("att", 3, 0), ("L", "S", 0, 3),
    ("U", "M", 0, -2), ("att", 3, 1), ("L", "M", 1, -3), ("L", "O", 0, -3), ("L", "S", 1, 2), ("U", "SO", 0, -1),
    ("U", "C", 0, 1), ("L", "Ob", 0, 4), ("att", 3, 2), ("U", "C", 1, 0), ("post",), ("L", "S", 0, -3), ("ff", 0),
    ("U", "SP", 0, 1), ("ff", 1), ("U", "C", 0, -1), ("U", "SP", 1, 0), ("L", "C", 1, -3), ("U", "M", 1, 2),
    ("U", "O", 1, 1), ("L", "Ma", 0, 4), ("ff", 2), ("L", "Mb", 1, 4), ("U", "M", 0, 3), ("ff", 3), ("U", "O", 1, -1),
    ("L", "Cb", 0, 4), ("U", "SP", 0, -1), ("L", "Ca", 0, 4), ("ff", 4), ("U", "SO", 1, 1), ("L", "C", 1, 3),
    ("ff", 5), ("ff", 6), ("U", "SO", 1, -1), ("ff", 7), ("end",), ("U", "O", 0, 2), ("U", "M", 1, -2),
    ("U", "O", 0, -2), ("L", "O", 1, 3), ("U", "M", 0, -3), ("U", "C", 0, 2), ("U", "SO", 0, 2), ("L", "Oa", 0, 4),
    ("U", "C", 1, 1), ("U", "SO", 0, -2), ("L", "O", 1, -3), ("L", "S", 1, 3), ("L", "Ma", 1, 4), ("U", "Mb", 0, 4),
    ("U", "SP", 0, 2), ("L", "S", 0, 4), ("U", "C", 1, -1), ("L", "Ca", 1, 4), ("U", "SP", 1, 1), ("L", "S", 1, -3),
    ("U", "C", 0, -2), ("U", "SP", 1, -1), ("U", "O", 1, 2), ("U", "O", 1, -2), ("L", "Ob", 1, 4), ("U", "SP", 0, -2),
    ("U", "Ma", 0, 4), ("U", "SO", 1, 2), ("U", "SO", 1, -2), ("U", "C", 0, 3), ("U", "M", 1, 3), ("U", "M", 1, -3),
    ("L", "Cb", 1, 4), ("U", "SP", 0, 3), ("U", "O", 0, -3), ("U", "O", 0, 3), ("L", "Oa", 1, 4), ("U", "SO", 0, -3),
    ("U", "C", 0, -3), ("U", "C", 1, -2), ("U", "SO", 0, 3), ("U", "Ob", 0, 4), ("U", "Cb", 0, 4), ("L", "S", 1, 4),
    ("lift", 0), ("U", "C", 1, 2), ("U", "Oa", 0, 4), ("lift", 1), ("U", "SP", 0, -3), ("U", "Ma", 1, 4),
    ("U", "SP", 1, -2), ("lift", 2), ("U", "Mb", 1, 4), ("U", "SP", 1, 2), ("lift", 3), ("U", "SO", 0, 4),
    ("up", 0, ()), ("U", "O", 1, -3), ("U", "Ca", 0, 4), ("U", "O", 1, 3), ("up", -1, ()), ("U", "C", 1, 3),
    ("U", "SO", 1, -3), ("U", "C", 1, -3), ("up", 1, ()), ("U", "Oa", 1, 4), ("U", "SP", 0, 4), ("U", "SO", 1, 3),
    ("U", "Ob", 1, 4), ("up", -2, (1,)), ("U", "SP", 1, 3), ("U", "Cb", 1, 4), ("U", "SP", 1, -3), ("U", "SO", 1, 4),
    ("U", "Ca", 1, 4), ("up", 2, (0,)), ("U", "SP", 1, 4), ("up", -3, (2,)), ("up", 3, (-1,)), ("early", 3), ("row",),
    ("up", 4, ()), ("last",),
)


def dot(a, b):
    return jnp.dot(a, b, preferred_element_type=F32)


def dot_nt(a, b):
    return lax.dot_general(a, b, (((1,), (1,)), ((), ())), preferred_element_type=F32)


def elu(v):
    return jnp.where(v > 0, v, jnp.exp(jnp.minimum(v, 0.0)) - 1.0)


def layer_norm(v, gain):
    centred = v - jnp.mean(v, axis=-1, keepdims=True)
    variance = jnp.mean(centred * centred, axis=-1, keepdims=True)
    return centred * lax.rsqrt(variance + 1e-05) * gain


def kernel(
    lat, ga, wq, wk, wv, wo, sa, gf, wup, wdn, sf, wl, bl, wu, bu, wc1, b1, wc2, b2, near, far,
    out,
    lbuf, ubuf, xin, vproj, vup, vdn, vc1, vc2, vga, vsa, vgf, vsf, vbl, vbu, vb1, vb2, vnear, vfar,
    normed, turn, qs, ks, vs, mixed, res, acc, cur7, act2, rect, part, ups, obf,
    send_sems, recv_sems, here_sems, out_sems,
):
    g = Gather(wl, wu, lbuf, ubuf, send_sems, recv_sems)
    t = lax.axis_index("tm")
    here = []

    def bring(src, dst):
        copy = pltpu.make_async_copy(src, dst, here_sems.at[len(here)])
        copy.start()
        here.append(copy)
        return copy

    own_x = bring(lat, xin.at[pl.ds(HALO, FRAMES)])
    in_ga, in_near, in_far = bring(ga, vga), bring(near, vnear), bring(far, vfar)
    g.barrier()
    g.event("L", "M", 0, 0)
    g.event("L", "C", 0, 0)
    g.start(lat, xin.at[pl.ds(LEAD, FRAMES)], g.after[0], 0)
    g.start(lat.at[pl.ds(FRAMES - LEAD, LEAD)], xin.at[pl.ds(0, LEAD)], g.after[1], 1)
    in_proj = [bring(w, vproj.at[i]) for i, w in enumerate((wk, wv, wq, wo))]
    own_l = bring(wl, g.ref("L", "W", 0, 0))
    own_u = bring(wu, g.ref("U", "W", 0, 0))
    in_up, in_dn = bring(wup, vup), bring(wdn, vdn)
    in_vec = [
        bring(a, b)
        for a, b in ((sa, vsa), (gf, vgf), (sf, vsf), (bl, vbl), (bu, vbu), (b1, vb1), (b2, vb2))
    ]
    in_c1, in_c2 = bring(wc1, vc1), bring(wc2, vc2)

    lane = lax.broadcasted_iota(jnp.int32, (1, 128), 1)
    first, low = lane % 64 < 32, lane < 64
    live_row = lax.broadcasted_iota(jnp.int32, (LIVE, 1), 0)
    real = (live_row >= LEAD) | (t > 0)
    tail = ROWS - LIVE

    def first_norm():
        own_x.wait()
        g.wait(xin.at[pl.ds(LEAD, FRAMES)], 0)
        g.wait(xin.at[pl.ds(0, LEAD)], 1)
        for copy in (in_ga, in_near, in_far):
            copy.wait()
        normed[...] = layer_norm(xin[...].astype(F32), vga[...]).astype(BF16)
        cos_a, sin_a = vfar[0, pl.ds(t, 1), :], vfar[1, pl.ds(t, 1), :]
        cos_b, sin_b = vnear[0], vnear[1]
        turn[0] = cos_a * cos_b - sin_a * sin_b
        sine = sin_a * cos_b + cos_a * sin_b
        turn[1] = jnp.where(first, -sine, sine)

    def rope(v, skip):
        parts = []
        for i in range(4):
            block = v[:, 128 * i : 128 * i + 128]
            other = jnp.where(first, pltpu.roll(block, 96, 1), pltpu.roll(block, 32, 1))
            parts.append(block * turn[0, skip:] + other * turn[1, skip:])
        return jnp.concatenate(parts, axis=1).astype(BF16)

    def keys():
        in_proj[0].wait()
        ks[...] = rope(dot(normed[...], vproj[0]), 0)

    def values():
        in_proj[1].wait()
        vs[...] = dot(normed[...], vproj[1]).astype(BF16)

    def queries():
        in_proj[2].wait()
        qs[...] = rope(dot(normed[tail:], vproj[2]), tail) * BF16(0.125)

    def attention(pair, block):
        lanes = slice(128 * pair, 128 * pair + 128)
        q0, size, k0, width = ((256, 96, 0, 352), (352, 96, 96, 352), (448, 80, 192, 336))[block]
        q_row = q0 + lax.broadcasted_iota(jnp.int32, (size, width), 0)
        k_row = k0 + lax.broadcasted_iota(jnp.int32, (size, width), 1)
        allowed = (k_row <= q_row) & (k_row > q_row - WIN) & (k_row >= HALO - FRAMES * t)
        q = qs[q0 - tail : q0 - tail + size, lanes]
        k, v = ks[k0 : k0 + width, lanes], vs[k0 : k0 + width, lanes]
        halves = []
        for mask in (low, ~low):
            scores = jnp.where(allowed, dot_nt(jnp.where(mask, q, BF16(0)), k), -1e30)
            weights = jnp.exp(scores - jnp.max(scores, axis=-1, keepdims=True))
            weights = jnp.where(allowed, weights, 0.0)
            total = jnp.maximum(jnp.sum(weights, axis=-1, keepdims=True), 0.5)
            halves.append(dot((weights / total).astype(BF16), v))
        mixed[q0 - tail : q0 - tail + size, lanes] = jnp.where(low, *halves).astype(BF16)

    def after_attention():
        in_proj[3].wait()
        for copy in in_vec:
            copy.wait()
        state = xin[tail:, :].astype(F32)
        residual = state + vsa[...] * dot(mixed[...], vproj[3])
        res[...] = residual
        normed[:LIVE] = layer_norm(residual, vgf[...]).astype(BF16)
        in_up.wait()
        in_dn.wait()

    def feed_forward(i):
        cols = slice(256 * i, 256 * i + 256)
        v = dot(normed[:LIVE], vup[:, cols])
        hidden = (0.5 * v * (1.0 + lax.erf(v * (1.0 / math.sqrt(2.0))))).astype(BF16)
        more = dot(hidden, vdn[cols, :])
        acc[...] = more if i == 0 else acc[...] + more

    def layer_end():
        current = (res[...] + vsf[...] * acc[...]).astype(BF16).astype(F32)
        current = jnp.where(real, current, 0.0)
        for m in range(7):
            moved = pltpu.roll(current, 6 - m, 0) if m < 6 else current
            cur7[:, 512 * m : 512 * m + 512] = moved.astype(BF16)

    def lift(i):
        if i == 0:
            own_l.wait()
        cols = slice(256 * i, 256 * i + 256)
        total = sum(dot_nt(cur7[:, 512 * m : 512 * m + 512], lbuf[m, cols, :]) for m in range(7)) + vbl[:, cols]
        active = jnp.where(real, elu(total), 0.0).astype(BF16)
        act2[:, cols] = active
        act2[:, C0 + 256 * i : C0 + 256 * i + 256] = pltpu.roll(active.astype(F32), 1, 0).astype(BF16)

    def phase(d):
        return (g.z + d + 8) % 8

    def tap(row, j, half):
        yl = (g.y + row) % 2
        return dot(act2[:, pl.ds(pl.multiple_of(C0 * yl, C0), C0)], ubuf[yl, j, half])

    def upsample(d, units):
        if d == 0:
            own_u.wait()
            in_c1.wait()
            in_c2.wait()
        for u in units:
            residual_unit(u)
        j = phase(d)
        for half in range(2):
            cols = slice(256 * half, 256 * half + 256)
            if d == 4:
                up = acc[:, cols] + tap(1, j, half)
            else:
                up = dot(act2[:, :C0], ubuf[0, j, half]) + dot(act2[:, C0:], ubuf[1, j, half])
            up = (up + vbu[:, cols]).astype(BF16)
            ups[j, :, cols] = up[LEAD:]
            rectified = elu(up.astype(F32)).astype(BF16)
            rect[j + 2, :LEAD, cols] = jnp.where(t > 0, rectified[:LEAD], BF16(0))
            rect[j + 2, LEAD:, cols] = rectified[LEAD:]

        @pl.when(j >= 6)
        def _():
            rect[j - 6] = pltpu.roll(rect[j + 2].astype(F32), 1, 0).astype(BF16)

    leaving = []
    last_tap = {4: 2, -3: 1, -2: 0}

    def conv(j, m):
        return dot(rect[j + m, LEAD:], vc1[:, CH * m : CH * m + CH])

    def last_begin(*units):
        for u in units:
            residual_unit(u)
        for u, last in last_tap.items():
            one, two = (m for m in range(3) if m != last)
            part[last] = vb1[...] + conv(phase(u), one) + conv(phase(u), two)

    def last_row():
        for half in range(2):
            acc[:, 256 * half : 256 * half + 256] = tap(0, phase(4), half)

    def residual_unit(d):
        j = phase(d)
        if d in last_tap:
            total = part[last_tap[d]] + conv(j, last_tap[d])
        else:
            total = vb1[...] + conv(j, 0) + conv(j, 1) + conv(j, 2)
        second = dot(elu(total).astype(BF16), vc2[...])
        obf[j] = (ups[j].astype(F32) + vb2[...] + second).astype(BF16)
        copy = pltpu.make_async_copy(obf.at[j], out.at[j], out_sems.at[len(leaving)])
        copy.start()
        leaving.append(copy)

    def last_units():
        for d in last_tap:
            residual_unit(d)

    steps = dict(
        norm=first_norm, k=keys, v=values, q=queries, att=attention, post=after_attention, ff=feed_forward,
        end=layer_end, lift=lift, up=upsample, early=last_begin, row=last_row, last=last_units,
    )
    for name, *where in PLAN:
        if name in steps:
            steps[name](*where)
        else:
            g.event(name, *where)
    for copy in leaving:
        copy.wait()
    g.finish()


def weave(phases, out, rows):
    for i in range(4):
        lanes = slice(128 * i, 128 * i + 128)
        for j in range(UPS):
            rows[i, pl.ds(j, phases.shape[1], stride=UPS), :] = phases[j, :, lanes].astype(F32)
        out[:, lanes] = rows[i].astype(BF16)


def tables():
    frequency = 10000.0 ** (-np.arange(32, dtype=np.float64) / 32)
    frequency = np.tile(frequency, 4)[None, :]

    def both(frames):
        angles = frames[:, None] * frequency
        return np.stack([np.cos(angles), np.sin(angles)]).astype(np.float32)

    return both(np.arange(ROWS) - float(HALO)), both(np.arange(32) * float(FRAMES))


def body(
    latents, gain_attn, w_query, w_key, w_value, w_out, scale_attn, gain_ffn, w_up, w_down, scale_ffn,
    w_lift, bias_lift, w_upsample, bias_upsample, w_conv_first, bias_first, w_conv_second, bias_second,
):
    near, far = tables()
    operands = (
        latents[0], gain_attn, w_query[0], w_key[0], w_value[0], w_out[0], scale_attn, gain_ffn, w_up[0], w_down[0],
        scale_ffn, jnp.transpose(w_lift, (0, 2, 1)), bias_lift[None], w_upsample, bias_upsample[None], w_conv_first,
        bias_first[None], w_conv_second, bias_second[None], jnp.asarray(near), jnp.asarray(far),
    )
    vmem = pltpu.VMEM
    dma = pltpu.SemaphoreType.DMA
    phases = pl.pallas_call(
        kernel,
        out_shape=jax.ShapeDtypeStruct((UPS, FRAMES, C1), BF16),
        in_specs=[pl.BlockSpec(memory_space=pl.ANY)] * len(operands),
        out_specs=pl.BlockSpec(memory_space=pl.ANY),
        scratch_shapes=[
            vmem((7, C0, D), BF16),
            vmem((2, UPS, 2, C0, C1 // 2), BF16),
            vmem((ROWS, D), BF16),
            vmem((4, D, D), BF16),
            vmem((D, FF), BF16),
            vmem((FF, D), BF16),
            vmem((C1, 3 * CH), BF16),
            vmem((CH, C1), BF16),
            vmem((1, D), F32),
            vmem((1, D), F32),
            vmem((1, D), F32),
            vmem((1, D), F32),
            vmem((1, C0), F32),
            vmem((1, C1), F32),
            vmem((1, CH), F32),
            vmem((1, C1), F32),
            vmem((2, ROWS, 128), F32),
            vmem((2, 32, 128), F32),
            vmem((ROWS, D), BF16),
            vmem((2, ROWS, 128), F32),
            vmem((LIVE, D), BF16),
            vmem((ROWS, D), BF16),
            vmem((ROWS, D), BF16),
            vmem((LIVE, D), BF16),
            vmem((LIVE, D), F32),
            vmem((LIVE, D), F32),
            vmem((LIVE, 7 * D), BF16),
            vmem((LIVE, 2 * C0), BF16),
            vmem((UPS + 2, LIVE, C1), BF16),
            vmem((3, FRAMES, CH), F32),
            vmem((UPS, FRAMES, C1), BF16),
            vmem((UPS, FRAMES, C1), BF16),
            dma((172,)),
            dma((172,)),
            dma((24,)),
            dma((8,)),
        ],
        compiler_params=pltpu.CompilerParams(collective_id=0, has_side_effects=True, vmem_limit_bytes=60 * 2**20),
        cost_estimate=pl.CostEstimate(flops=11 * 10**9, bytes_accessed=36 * 10**6, transcendentals=4 * 10**6),
    )(*operands)
    block = 128
    result = pl.pallas_call(
        weave,
        out_shape=jax.ShapeDtypeStruct((FRAMES * UPS, C1), BF16),
        grid=(FRAMES // block,),
        in_specs=[pl.BlockSpec((UPS, block, C1), lambda i: (0, i, 0))],
        out_specs=pl.BlockSpec((UPS * block, C1), lambda i: (i, 0)),
        scratch_shapes=[vmem((4, UPS * block, 128), F32)],
    )(phases)
    return result[None]


def solution(mesh):
    whole = P()
    placed = [whole] * 19
    placed[0] = P("stream", "tm", None)
    placed[11] = P(None, None, "tm")
    placed[13] = P(None, "tm")
    return jax.shard_map(
        body, mesh=mesh, in_specs=tuple(placed), out_specs=P("stream", "tm", None), check_vma=False
    )
```
